32 devices in a mesh: dp: 16 (over z, y, core), grp: 2 (over x).
Axes of the slice: x: 2, y: 2, z: 4, core: 2. Of those that a mesh axis runs over, the one named last changes fastest.
Arguments:
- feature_maps: bfloat16 [2, 32, 56, 3584], P(None, ('dp', 'grp')), may hold values from -200 to 200, as said below
- output_grads: bfloat16 [2, 32, 56, 3584], P(None, ('dp', 'grp')), may hold values from -200 to 200, as said below
Outputs:
- precond: float32 [2, 64, 576], replicated
The draws below stay inside these ranges and needn't reach their ends.
Inputs may be any that keep to these rules, and one draw needn't show every extreme that they name: `feature_maps`: real values. `output_grads`: real values.
All inputs are finite; a program needn't handle non-finite values.
Results may differ from the reference program's by a relative error of at most 0.0003.
Values sent between devices are 32-bit elements; how exact they have to be, the bound alone decides.
No kernel may reach another device: no remote copies, remote signals or barrier semaphores. Data moves between devices by JAX's collectives and lax.ppermute only.
A program may use at most 128 MiB of HBM per device.

```python
import math
import jax
import jax.numpy as jnp
from jax import lax

C = 64
PATCH = 576
MAP_W = 56
MAP_H = 56
L = 2
NS_ITERS = 2
IMAGES = 32
ROWS_TOTAL = 100352


def shared_fields(key):
    base_key = jax.random.fold_in(key, 7)
    keys = jax.random.split(base_key, 8)
    shape_five = (L, IMAGES, MAP_H, MAP_W, C)
    rough = jnp.clip(jax.random.normal(keys[0], shape_five, jnp.float32), -5.0, 5.0)
    field = jnp.clip(jax.random.normal(keys[1], (L, IMAGES, MAP_H + 2, MAP_W + 2, C), jnp.float32), -5.0, 5.0)
    smooth = jnp.zeros(shape_five, jnp.float32)
    for row_tap in range(3):
        for col_tap in range(3):
            smooth = smooth + field[:, :, row_tap:row_tap + MAP_H, col_tap:col_tap + MAP_W, :]
    smooth = smooth / 3.0
    common = jnp.clip(jax.random.normal(keys[2], (L, IMAGES, MAP_H, MAP_W, 1), jnp.float32), -5.0, 5.0)
    channel_scale = jnp.exp(jax.random.uniform(keys[3], (L, 1, 1, 1, C), jnp.float32, 0.0, math.log(3.2)))
    image_scale = jnp.exp(jax.random.uniform(keys[4], (L, IMAGES, 1, 1, 1), jnp.float32, 0.0, math.log(3.0)))
    channel_level = jax.random.uniform(keys[7], (L, 1, 1, 1, C), jnp.float32, 0.3, 0.7)
    row_place = jnp.arange(MAP_H).reshape(1, 1, MAP_H, 1, 1)
    col_place = jnp.arange(MAP_W).reshape(1, 1, 1, MAP_W, 1)
    on_edge = (row_place == 0) | (row_place == MAP_H - 1) | (col_place == 0) | (col_place == MAP_W - 1)
    border_gain = jnp.where(on_edge, 2.0, 1.0).astype(jnp.float32)
    maps = 0.5 * image_scale * channel_scale * border_gain * (0.8 * rough + 0.8 * smooth + 0.4 * common + channel_level)
    noise = jnp.clip(jax.random.normal(keys[5], shape_five, jnp.float32), -5.0, 5.0)
    grad_scale = jnp.exp(jax.random.uniform(keys[6], (L, 1, 1, 1, C), jnp.float32, 0.0, math.log(3.2)))
    grads = 0.5 * maps + 0.5 * grad_scale * noise
    return (maps.reshape(L, IMAGES, MAP_H, MAP_W * C), grads.reshape(L, IMAGES, MAP_H, MAP_W * C))


def draw_feature_maps(key, part):
    return shared_fields(key)[0].astype(jnp.bfloat16)


def draw_output_grads(key, part):
    return shared_fields(key)[1].astype(jnp.bfloat16)


def setup_inputs(seed: int = 0) -> dict:
    key_list = jax.random.split(jax.random.key(seed), 3)
    feature_maps = draw_feature_maps(jax.random.fold_in(key_list[2], 71), 0)
    output_grads = draw_output_grads(jax.random.fold_in(key_list[2], 71), 0)
    return dict(feature_maps=feature_maps, output_grads=output_grads)


damping_factor = 0.1

def patch_rows(feature):
    height = feature.shape[0]
    cube = feature.reshape(height, MAP_W, C)
    padded = jnp.pad(cube, ((1, 1), (1, 1), (0, 0)))
    pieces = [padded[row_tap:row_tap + height, col_tap:col_tap + MAP_W, :] for row_tap in range(3) for col_tap in range(3)]
    return jnp.concatenate(pieces, axis=-1).reshape(height * MAP_W, 9 * C)

def damped(factor):
    size_n = factor.shape[-1]
    identity_mat = jnp.eye(size_n, dtype=jnp.float32)
    return factor + damping_factor * jnp.trace(factor) / size_n * identity_mat

def newton_inverse(matrix):
    size_n = matrix.shape[-1]
    identity_mat = jnp.eye(size_n, dtype=jnp.float32)
    current = identity_mat / jnp.sqrt(jnp.sum(matrix * matrix))
    for sweep in range(NS_ITERS):
        product = jnp.dot(matrix, current, precision=lax.Precision.HIGHEST)
        current = jnp.dot(current, 2.0 * identity_mat - product, precision=lax.Precision.HIGHEST)
    return current

def precondition(cov_a, cov_g, grad_w):
    inverse_a = newton_inverse(damped(cov_a))
    inverse_g = newton_inverse(damped(cov_g))
    left = jnp.dot(inverse_g, grad_w, precision=lax.Precision.HIGHEST)
    return jnp.dot(left, inverse_a, precision=lax.Precision.HIGHEST)

def reference(feature_maps, output_grads):
    results = []
    for layer_index in range(L):

        def accumulate(carry, pair):
            feature, gradient = pair
            patches = patch_rows(feature).astype(jnp.float32)
            grads = gradient.reshape(-1, C).astype(jnp.float32)
            sum_a = carry[0] + jnp.dot(patches.T, patches, precision=lax.Precision.HIGHEST)
            sum_g = carry[1] + jnp.dot(grads.T, grads, precision=lax.Precision.HIGHEST)
            sum_w = carry[2] + jnp.dot(grads.T, patches, precision=lax.Precision.HIGHEST)
            return ((sum_a, sum_g, sum_w), None)
        start = (jnp.zeros((PATCH, PATCH), jnp.float32), jnp.zeros((C, C), jnp.float32), jnp.zeros((C, PATCH), jnp.float32))
        totals, unused = lax.scan(accumulate, start, (feature_maps[layer_index], output_grads[layer_index]))
        scale = 1.0 / ROWS_TOTAL
        results.append(precondition(totals[0] * scale, totals[1] * scale, totals[2] * scale))
    return jnp.stack(results)
```

```python
import functools

import jax
import jax.numpy as jnp
import numpy as np
from jax import lax
from jax.experimental import pallas as pl
from jax.experimental.pallas import tpu as pltpu
from jax.sharding import PartitionSpec as P

C = 64
TAPS = 9
PAIR = 2 * C
ROW = 64
NPAIR = 20
QUART = 5
DAMP = 0.1
F32 = jnp.float32
BF16 = jnp.bfloat16

PAIRS = (
    "x1m", "x1z", "cc1", "x2m", "x2z",
    "cc2", "x22", "x0z", "cc0", "r0z",
    "r1z", "k0", "k1", "w0z", "w1z",
    "w2z", "h0", "h1", "h2", "gg",
)
PLACE = {name: index for index, name in enumerate(PAIRS)}


def contract0(a, b):
    return lax.dot_general(a, b, (((0,), (0,)), ((), ())), preferred_element_type=F32)


def chip_place():
    dp = lax.axis_index("dp")
    core = lax.rem(dp, 2)
    second = lax.rem(dp // 2, 2)
    first = lax.axis_index("grp")
    return core, first, second


def slot_of(quarter, layer, first, second):
    mine_first = first ^ (quarter // 2)
    mine_second = second ^ (quarter % 2)
    major = jnp.where(layer == 0, mine_first, mine_second)
    minor = jnp.where(layer == 0, mine_second, mine_first)
    return 2 * major + minor


def local_kernel(height, width, x_hbm, g_hbm, send_ref, keep_ref, xbuf, gbuf, shifted, lhs_t, edges, sems):
    core, first, second = chip_place()
    wp = width // 2
    rows = wp * ROW
    layers = [1 - core, core]
    copies = []
    for i in range(2):
        copies.append(
            (
                pltpu.make_async_copy(x_hbm.at[layers[i], 0], xbuf.at[i], sems.at[2 * i]),
                pltpu.make_async_copy(g_hbm.at[layers[i], 0], gbuf.at[i], sems.at[2 * i + 1]),
            )
        )
    for pair in copies:
        for one in pair:
            one.start()
    for d in range(4):
        shifted[d, 0:ROW, :] = jnp.zeros((ROW, PAIR), BF16)
        shifted[d, ROW + rows : 2 * ROW + rows, :] = jnp.zeros((ROW, PAIR), BF16)
    edges[...] = jnp.zeros_like(edges)
    low = lax.broadcasted_iota(jnp.int32, (ROW, PAIR), 1) < C
    pad = jnp.zeros((ROW - height, PAIR), F32)
    n_edge = edges.shape[1] - 16

    for i in range(2):
        layer = layers[i]
        copies[i][0].wait()
        copies[i][1].wait()
        for pair in range(wp // 2):
            tiles_x = []
            tiles_g = []
            for half in range(2):
                j = 2 * pair + half
                block = jnp.concatenate([xbuf[i, :, j * PAIR : (j + 1) * PAIR].astype(F32), pad], axis=0)
                at = ROW + j * ROW
                edges[0, 8 + j : 9 + j, :] = block[0:1, :]
                edges[1, 8 + j : 9 + j, :] = block[height - 1 : height, :]
                shifted[0, at : at + ROW, :] = pltpu.roll(block, 1, 0).astype(BF16)
                shifted[1, at : at + ROW, :] = block.astype(BF16)
                shifted[2, at : at + ROW, :] = pltpu.roll(block, ROW - 1, 0).astype(BF16)
                shifted[3, at : at + ROW, :] = pltpu.roll(block, ROW - 2, 0).astype(BF16)
                tiles_x.append(block)
                tiles_g.append(jnp.concatenate([gbuf[i, :, j * PAIR : (j + 1) * PAIR].astype(F32), pad], axis=0))
            lanes = slice(pair * PAIR, (pair + 1) * PAIR)
            lhs_t[0:PAIR, lanes] = jnp.concatenate(tiles_x, axis=0).T.astype(BF16)
            lhs_t[PAIR : 2 * PAIR, lanes] = jnp.concatenate(tiles_g, axis=0).T.astype(BF16)

        def product(d, s, part):
            left = lhs_t[...] if part is None else lhs_t[part * PAIR : (part + 1) * PAIR, :]
            right = [shifted[d, (1 + one) * ROW : (1 + one) * ROW + rows, :] for one in s]
            right = right[0] if len(right) == 1 else jnp.concatenate(right, axis=1)
            full = jnp.dot(left, right, preferred_element_type=F32)
            return [full[:, k * PAIR : (k + 1) * PAIR] for k in range(len(s))]

        def table(at_s, base, s):
            upper = at_s[s][base : base + C, :]
            here = pltpu.roll(at_s[s][base + C : base + PAIR, :], C, 1)
            if s + 1 not in at_s:
                return upper + here
            after = pltpu.roll(at_s[s + 1][base + C : base + PAIR, :], C, 1)
            return upper + jnp.where(low, here, after)

        def odd(at_s, base, s):
            return at_s[s][base : base + C, :] + pltpu.roll(at_s[s + 1][base + C : base + PAIR, :], C, 1)

        def store(name, value):
            index = PLACE[name]
            slot = slot_of(index // QUART, layer, first, second)
            (send_ref if i == 0 else keep_ref)[slot, index % QUART] = value

        p = product(0, (-1, 0), 1) + product(0, (1,), 1)
        at_s = dict(zip((-1, 0, 1), p))
        store("w0z", table(at_s, 0, 0))
        w0 = odd(at_s, 0, -1)
        p = product(1, (-1, 0), None) + product(1, (1,), None)
        at_s = dict(zip((-1, 0, 1), p))
        store("x0z", table(at_s, 0, 0))
        store("h0", jnp.where(low, table(at_s, 0, 1), w0))
        store("w1z", table(at_s, PAIR, 0))
        w1 = odd(at_s, PAIR, -1)
        p = product(2, (-1, 0), None) + product(2, (1,), None)
        at_s = dict(zip((-1, 0, 1), p))
        store("x1m", table(at_s, 0, -1))
        store("x1z", table(at_s, 0, 0))
        x12 = table(at_s, 0, 1)
        store("w2z", table(at_s, PAIR, 0))
        w2 = odd(at_s, PAIR, -1)
        p = product(3, (-1, 0), 0) + product(3, (1,), 0)
        at_s = dict(zip((-1, 0, 1), p))
        store("x2m", table(at_s, 0, -1))
        store("x2z", table(at_s, 0, 0))
        store("x22", jnp.where(low, x12, pltpu.roll(table(at_s, 0, 1), C, 1)))
        gl = lhs_t[PAIR : 2 * PAIR, :]
        gg = lax.dot_general(gl, gl, (((1,), (1,)), ((), ())), preferred_element_type=F32)
        store("gg", gg[0:C, :] + pltpu.roll(gg[C:PAIR, :], C, 1))
        fl = [
            jnp.where(
                low,
                shifted[d, ROW : 2 * ROW, :].astype(F32),
                shifted[d, rows : ROW + rows, :].astype(F32),
            ).astype(BF16)
            for d in (1, 2, 3)
        ]
        for d, name in enumerate(("cc0", "cc1", "cc2")):
            q = contract0(fl[0], fl[d])
            store(name, jnp.where(low, q[0:C, :], q[C:PAIR, :]))
        line = lax.broadcasted_iota(jnp.int32, (n_edge, PAIR), 0)
        lane = lax.broadcasted_iota(jnp.int32, (n_edge, PAIR), 1)
        corner = ((line == 0) & (lane < C)) | ((line == wp - 1) & (lane >= C))
        halves = []
        for e in range(2):
            zero = edges[e, 8 : 8 + n_edge, :]
            here = zero.astype(BF16)
            after = edges[e, 9 : 9 + n_edge, :].astype(BF16)
            at_s = {0: contract0(here, here), 1: contract0(here, after)}
            store(("r0z", "r1z")[e], table(at_s, 0, 0))
            halves.append(table(at_s, 0, 1))
            only = jnp.where(corner, zero, 0.0).astype(BF16)
            q = contract0(only, only)
            store(("k0", "k1")[e], jnp.where(low, q[0:C, :], q[C:PAIR, :]))
        store("h1", jnp.where(low, halves[0], w1))
        store("h2", jnp.where(low, halves[1], w2))


def local_sums(feature_maps, output_grads):
    height = feature_maps.shape[2]
    width = feature_maps.shape[3] // C
    wp = width // 2
    shape = jax.ShapeDtypeStruct((4, QUART, C, PAIR), F32)
    n_edge = (wp + 15) // 16 * 16
    return pl.pallas_call(
        functools.partial(local_kernel, height, width),
        out_shape=(shape, shape),
        in_specs=[pl.BlockSpec(memory_space=pl.ANY)] * 2,
        out_specs=(pl.BlockSpec(memory_space=pltpu.VMEM),) * 2,
        scratch_shapes=[
            pltpu.VMEM((2, height, width * C), BF16),
            pltpu.VMEM((2, height, width * C), BF16),
            pltpu.VMEM((4, (wp + 2) * ROW, PAIR), BF16),
            pltpu.VMEM((2 * PAIR, wp * ROW), BF16),
            pltpu.VMEM((2, n_edge + 16, PAIR), F32),
            pltpu.SemaphoreType.DMA((4,)),
        ],
        compiler_params=pltpu.CompilerParams(vmem_limit_bytes=40 * 2**20),
    )(feature_maps, output_grads)


def split(a):
    high = a.astype(BF16)
    return high, (a - high.astype(F32)).astype(BF16)


def dot3(a, b):
    ah, al = split(a)
    bh, bl = split(b)
    dot = functools.partial(jnp.dot, preferred_element_type=F32)
    return dot(ah, bh) + (dot(ah, bl) + dot(al, bh))


def normalized(m):
    n = m.shape[0]
    diag = lax.broadcasted_iota(jnp.int32, (n, n), 0) == lax.broadcasted_iota(jnp.int32, (n, n), 1)
    trace = jnp.sum(jnp.where(diag, m, 0.0))
    m = m + jnp.where(diag, DAMP * trace / n, 0.0)
    inv = lax.rsqrt(jnp.sum(m * m))
    return jnp.where(diag, 1.0, 0.0) - m * inv, inv


def final_kernel(total_rows, near_ref, far_ref, out_ref, quarters, m_ref, e_hi, e_lo):
    core, first, second = chip_place()
    quarters[0:2] = near_ref[...]
    quarters[2:4] = far_ref[...]

    def load(name):
        index = PLACE[name]
        both = quarters[slot_of(index // QUART, core, first, second), index % QUART]
        return both[:, 0:C], both[:, C:PAIR]

    x0 = dict(zip((0, 1), load("x0z")))
    h0, w00 = load("h0")
    x0[2] = h0
    row0 = dict(zip((0, 1), load("r0z")))
    row0[2], w10 = load("h1")
    row1 = dict(zip((0, 1), load("r1z")))
    row1[2], w20 = load("h2")
    col0 = {}
    col1 = {}
    col0[0], col1[0] = load("cc0")
    corner = load("k0") + load("k1")
    down = {}
    for dr in (1, 2):
        down[dr, -2], down[dr, -1] = load("x%dm" % dr)
        down[dr, 0], down[dr, 1] = load("x%dz" % dr)
        col0[dr], col1[dr] = load("cc%d" % dr)
    down[1, 2], down[2, 2] = load("x22")

    def put(t, u, block):
        m_ref[t * C : (t + 1) * C, u * C : (u + 1) * C] = block

    def put_all(taps, block):
        for t, u in taps:
            put(t, u, block)
        flipped = block.T
        for t, u in taps:
            put(u, t, flipped)

    for a in range(3):
        line = {}
        for dc in range(3):
            line[dc] = x0[dc] - row1[dc] if a == 0 else (x0[dc] - row0[dc] if a == 2 else x0[dc])
        for b in range(3):
            block = line[0]
            if b == 0:
                block = block - col1[0]
                if a == 0:
                    block = block + corner[3]
                if a == 2:
                    block = block + corner[1]
            if b == 2:
                block = block - col0[0]
                if a == 0:
                    block = block + corner[2]
                if a == 2:
                    block = block + corner[0]
            put(3 * a + b, 3 * a + b, block)
        put_all([(3 * a, 3 * a + 1), (3 * a + 1, 3 * a + 2)], line[1])
        put_all([(3 * a, 3 * a + 2)], line[2])
    for dr in (1, 2):
        starts = range(3 - dr)
        for b in range(3):
            block = down[dr, 0]
            if b == 0:
                block = block - col1[dr]
            if b == 2:
                block = block - col0[dr]
            put_all([(3 * a + b, 3 * (a + dr) + b) for a in starts], block)
        for dc in (-2, -1, 1, 2):
            taps = [(3 * a + b, 3 * (a + dr) + b + dc) for a in starts for b in range(3) if 0 <= b + dc < 3]
            put_all(taps, down[dr, dc])

    e, inv_a = normalized(m_ref[...])
    hi, lo = split(e)
    e_hi[...] = hi
    e_lo[...] = lo
    g, _ = load("gg")
    eg, inv_g = normalized(g)
    eg2 = dot3(eg, eg)
    pg = eg + dot3(eg, eg2) + eg2
    w0 = load("w0z")
    w1 = load("w1z")
    w2 = load("w2z")
    w = jnp.concatenate([w00, w0[0], w0[1], w10, w1[0], w1[1], w20, w2[0], w2[1]], axis=1)
    w = w + dot3(pg, w)
    v = w.T * (inv_a * inv_g * total_rows)

    def apply(v):
        vh, vl = split(v)
        both = jnp.dot(e_hi[...], jnp.concatenate([vh, vl], axis=1), preferred_element_type=F32)
        return both[:, 0:C] + (both[:, C:PAIR] + jnp.dot(e_lo[...], vh, preferred_element_type=F32))

    v = v + apply(v)
    v = v + apply(apply(v))
    out_ref[...] = v.T


def precondition(near, far, total_rows):
    n = TAPS * C
    return pl.pallas_call(
        functools.partial(final_kernel, float(total_rows)),
        out_shape=jax.ShapeDtypeStruct((C, n), F32),
        in_specs=[pl.BlockSpec(memory_space=pltpu.VMEM)] * 2,
        out_specs=pl.BlockSpec(memory_space=pltpu.VMEM),
        scratch_shapes=[
            pltpu.VMEM((4, QUART, C, PAIR), F32),
            pltpu.VMEM((n, n), F32),
            pltpu.VMEM((n, n), BF16),
            pltpu.VMEM((n, n), BF16),
        ],
        compiler_params=pltpu.CompilerParams(vmem_limit_bytes=40 * 2**20),
    )(near, far)


def stages(n_dp, n_grp):
    n = n_dp * n_grp
    core_bit = n_grp
    halvings = [1, 2 * n_grp]
    rest = []
    bit = 4 * n_grp
    while bit < n:
        rest.append(bit)
        bit *= 2
    orders = (halvings + rest, halvings[::-1] + rest[::-1])
    pairing = []
    for k in range(len(orders[0])):
        pairing.append([(i, i ^ orders[1 if i & core_bit else 0][k]) for i in range(n)])
    return [(i, i ^ core_bit) for i in range(n)], pairing


def shards(feature_maps, output_grads):
    n_dp, n_grp = lax.axis_size("dp"), lax.axis_size("grp")
    cores, pairing = stages(n_dp, n_grp)
    swap = lambda a, p: lax.ppermute(a, ("dp", "grp"), p)
    total_rows = feature_maps.shape[2] * feature_maps.shape[3] // C * feature_maps.shape[1] * n_dp * n_grp
    send, keep = local_sums(feature_maps, output_grads)
    got = swap(send, cores)
    got_far = swap(keep[2:4] + got[2:4], pairing[0])
    got_next = swap(keep[1] + got[1] + got_far[1], pairing[1])
    own = keep[0] + got[0] + got_far[0] + got_next
    for p in pairing[2:]:
        own = own + swap(own, p)
    near = jnp.stack([own, swap(own, pairing[1])])
    far = swap(near, pairing[0])
    mine = precondition(near, far, total_rows)
    other = swap(mine, cores)
    core = lax.rem(lax.axis_index("dp"), 2)
    return jnp.where(core == 0, jnp.stack([mine, other]), jnp.stack([other, mine]))


def solution(mesh):
    placed = (P(None, ("dp", "grp"), None, None), P(None, ("dp", "grp"), None, None))
    return jax.shard_map(shards, mesh=mesh, in_specs=placed, out_specs=P(), check_vma=False)
```

```python
import functools

import jax
import jax.numpy as jnp
import numpy as np
from jax import lax
from jax.experimental import pallas as pl
from jax.experimental.pallas import tpu as pltpu
from jax.sharding import PartitionSpec as P

C = 64
TAPS = 9
PAIR = 2 * C
ROW = 64
QUART = 5
DAMP = 0.1
VMEM_LIMIT = 48 * 2**20
F32 = jnp.float32
BF16 = jnp.bfloat16

PAIRS = (
    "x1m", "x1z", "cc1", "x2m", "x2z",
    "cc2", "x22", "x0z", "cc0", "r0z",
    "r1z", "k0", "k1", "w0z", "w1z",
    "w2z", "h0", "h1", "h2", "gg",
)
PLACE = {name: index for index, name in enumerate(PAIRS)}


def contract0(a, b):
    return lax.dot_general(a, b, (((0,), (0,)), ((), ())), preferred_element_type=F32)


def chip_place():
    dp = lax.axis_index("dp")
    core = lax.rem(dp, 2)
    second = lax.rem(dp // 2, 2)
    first = lax.axis_index("grp")
    return core, first, second


def slot_of(quarter, layer, first, second):
    mine_first = first ^ (quarter // 2)
    mine_second = second ^ (quarter % 2)
    major = jnp.where(layer == 0, mine_first, mine_second)
    minor = jnp.where(layer == 0, mine_second, mine_first)
    return 2 * major + minor


def gathered_slot(quarter, first, second):
    return 2 * (second ^ (quarter % 2)) + (first ^ (quarter // 2))


def local_kernel(height, width, own, x_hbm, g_hbm, out_ref, xbuf, gbuf, shifted, lhs_t, edges, sems):
    core, first, second = chip_place()
    wp = width // 2
    rows = wp * ROW
    layer = core if own else 1 - core
    copy_x = pltpu.make_async_copy(x_hbm.at[layer, 0], xbuf, sems.at[0])
    copy_g = pltpu.make_async_copy(g_hbm.at[layer, 0], gbuf, sems.at[1])
    copy_x.start()
    copy_g.start()
    for d in range(4):
        shifted[d, 0:ROW, :] = jnp.zeros((ROW, PAIR), BF16)
        shifted[d, ROW + rows : 2 * ROW + rows, :] = jnp.zeros((ROW, PAIR), BF16)
    edges[...] = jnp.zeros_like(edges)
    low = lax.broadcasted_iota(jnp.int32, (ROW, PAIR), 1) < C
    pad = jnp.zeros((ROW - height, PAIR), F32)
    n_edge = edges.shape[1] - 16
    copy_x.wait()
    copy_g.wait()
    for pair in range(wp // 2):
        tiles_x = []
        tiles_g = []
        for half in range(2):
            j = 2 * pair + half
            block = jnp.concatenate([xbuf[:, j * PAIR : (j + 1) * PAIR].astype(F32), pad], axis=0)
            at = ROW + j * ROW
            edges[0, 8 + j : 9 + j, :] = block[0:1, :]
            edges[1, 8 + j : 9 + j, :] = block[height - 1 : height, :]
            shifted[0, at : at + ROW, :] = pltpu.roll(block, 1, 0).astype(BF16)
            shifted[1, at : at + ROW, :] = block.astype(BF16)
            shifted[2, at : at + ROW, :] = pltpu.roll(block, ROW - 1, 0).astype(BF16)
            shifted[3, at : at + ROW, :] = pltpu.roll(block, ROW - 2, 0).astype(BF16)
            tiles_x.append(block)
            tiles_g.append(jnp.concatenate([gbuf[:, j * PAIR : (j + 1) * PAIR].astype(F32), pad], axis=0))
        lanes = slice(pair * PAIR, (pair + 1) * PAIR)
        lhs_t[0:PAIR, lanes] = jnp.concatenate(tiles_x, axis=0).T.astype(BF16)
        lhs_t[PAIR : 2 * PAIR, lanes] = jnp.concatenate(tiles_g, axis=0).T.astype(BF16)

    def product(d, s, part):
        left = lhs_t[...] if part is None else lhs_t[part * PAIR : (part + 1) * PAIR, :]
        right = [shifted[d, (1 + one) * ROW : (1 + one) * ROW + rows, :] for one in s]
        right = right[0] if len(right) == 1 else jnp.concatenate(right, axis=1)
        full = jnp.dot(left, right, preferred_element_type=F32)
        return [full[:, k * PAIR : (k + 1) * PAIR] for k in range(len(s))]

    def table(at_s, base, s):
        upper = at_s[s][base : base + C, :]
        here = pltpu.roll(at_s[s][base + C : base + PAIR, :], C, 1)
        if s + 1 not in at_s:
            return upper + here
        after = pltpu.roll(at_s[s + 1][base + C : base + PAIR, :], C, 1)
        return upper + jnp.where(low, here, after)

    def odd(at_s, base, s):
        return at_s[s][base : base + C, :] + pltpu.roll(at_s[s + 1][base + C : base + PAIR, :], C, 1)

    def store(name, value):
        index = PLACE[name]
        slot = slot_of(index // QUART, layer, first, second)
        out_ref[slot, index % QUART] = value

    p = product(0, (-1, 0), 1) + product(0, (1,), 1)
    at_s = dict(zip((-1, 0, 1), p))
    store("w0z", table(at_s, 0, 0))
    w0 = odd(at_s, 0, -1)
    p = product(1, (-1, 0), None) + product(1, (1,), None)
    at_s = dict(zip((-1, 0, 1), p))
    store("x0z", table(at_s, 0, 0))
    store("h0", jnp.where(low, table(at_s, 0, 1), w0))
    store("w1z", table(at_s, PAIR, 0))
    w1 = odd(at_s, PAIR, -1)
    p = product(2, (-1, 0), None) + product(2, (1,), None)
    at_s = dict(zip((-1, 0, 1), p))
    store("x1m", table(at_s, 0, -1))
    store("x1z", table(at_s, 0, 0))
    x12 = table(at_s, 0, 1)
    store("w2z", table(at_s, PAIR, 0))
    w2 = odd(at_s, PAIR, -1)
    p = product(3, (-1, 0), 0) + product(3, (1,), 0)
    at_s = dict(zip((-1, 0, 1), p))
    store("x2m", table(at_s, 0, -1))
    store("x2z", table(at_s, 0, 0))
    store("x22", jnp.where(low, x12, pltpu.roll(table(at_s, 0, 1), C, 1)))
    gl = lhs_t[PAIR : 2 * PAIR, :]
    gg = lax.dot_general(gl, gl, (((1,), (1,)), ((), ())), preferred_element_type=F32)
    store("gg", gg[0:C, :] + pltpu.roll(gg[C:PAIR, :], C, 1))
    fl = [
        jnp.where(
            low,
            shifted[d, ROW : 2 * ROW, :].astype(F32),
            shifted[d, rows : ROW + rows, :].astype(F32),
        ).astype(BF16)
        for d in (1, 2, 3)
    ]
    for d, name in enumerate(("cc0", "cc1", "cc2")):
        q = contract0(fl[0], fl[d])
        store(name, jnp.where(low, q[0:C, :], q[C:PAIR, :]))
    line = lax.broadcasted_iota(jnp.int32, (n_edge, PAIR), 0)
    lane = lax.broadcasted_iota(jnp.int32, (n_edge, PAIR), 1)
    corner = ((line == 0) & (lane < C)) | ((line == wp - 1) & (lane >= C))
    halves = []
    for e in range(2):
        zero = edges[e, 8 : 8 + n_edge, :]
        here = zero.astype(BF16)
        after = edges[e, 9 : 9 + n_edge, :].astype(BF16)
        at_s = {0: contract0(here, here), 1: contract0(here, after)}
        store(("r0z", "r1z")[e], table(at_s, 0, 0))
        halves.append(table(at_s, 0, 1))
        only = jnp.where(corner, zero, 0.0).astype(BF16)
        q = contract0(only, only)
        store(("k0", "k1")[e], jnp.where(low, q[0:C, :], q[C:PAIR, :]))
    store("h1", jnp.where(low, halves[0], w1))
    store("h2", jnp.where(low, halves[1], w2))


def local_sums(feature_maps, output_grads, own):
    height = feature_maps.shape[2]
    width = feature_maps.shape[3] // C
    wp = width // 2
    shape = jax.ShapeDtypeStruct((4, QUART, C, PAIR), F32)
    n_edge = (wp + 15) // 16 * 16
    return pl.pallas_call(
        functools.partial(local_kernel, height, width, own),
        out_shape=shape,
        in_specs=[pl.BlockSpec(memory_space=pltpu.HBM)] * 2,
        out_specs=pl.BlockSpec(memory_space=pltpu.VMEM),
        scratch_shapes=[
            pltpu.VMEM((height, width * C), BF16),
            pltpu.VMEM((height, width * C), BF16),
            pltpu.VMEM((4, (wp + 2) * ROW, PAIR), BF16),
            pltpu.VMEM((2 * PAIR, wp * ROW), BF16),
            pltpu.VMEM((2, n_edge + 16, PAIR), F32),
            pltpu.SemaphoreType.DMA((2,)),
        ],
        compiler_params=pltpu.CompilerParams(vmem_limit_bytes=VMEM_LIMIT),
    )(feature_maps, output_grads)


def split(a):
    high = a.astype(BF16)
    return high, (a - high.astype(F32)).astype(BF16)


def dot3(a, b):
    ah, al = split(a)
    bh, bl = split(b)
    dot = functools.partial(jnp.dot, preferred_element_type=F32)
    return dot(ah, bh) + (dot(ah, bl) + dot(al, bh))


def normalized(m):
    n = m.shape[0]
    diag = lax.broadcasted_iota(jnp.int32, (n, n), 0) == lax.broadcasted_iota(jnp.int32, (n, n), 1)
    trace = jnp.sum(jnp.where(diag, m, 0.0))
    m = m + jnp.where(diag, DAMP * trace / n, 0.0)
    inv = lax.rsqrt(jnp.sum(m * m))
    return jnp.where(diag, 1.0, 0.0) - m * inv, inv


def final_kernel(total_rows, near_ref, far_ref, out_ref, quarters, m_ref, e_hi, e_lo):
    _, first, second = chip_place()
    quarters[0:2] = near_ref[...]
    quarters[2:4] = far_ref[...]

    def load(name):
        index = PLACE[name]
        both = quarters[gathered_slot(index // QUART, first, second), index % QUART]
        return both[:, 0:C], both[:, C:PAIR]

    x0 = dict(zip((0, 1), load("x0z")))
    h0, w00 = load("h0")
    x0[2] = h0
    row0 = dict(zip((0, 1), load("r0z")))
    row0[2], w10 = load("h1")
    row1 = dict(zip((0, 1), load("r1z")))
    row1[2], w20 = load("h2")
    col0 = {}
    col1 = {}
    col0[0], col1[0] = load("cc0")
    corner = load("k0") + load("k1")
    down = {}
    for dr in (1, 2):
        down[dr, -2], down[dr, -1] = load("x%dm" % dr)
        down[dr, 0], down[dr, 1] = load("x%dz" % dr)
        col0[dr], col1[dr] = load("cc%d" % dr)
    down[1, 2], down[2, 2] = load("x22")

    def put(t, u, block):
        m_ref[t * C : (t + 1) * C, u * C : (u + 1) * C] = block

    def put_all(taps, block):
        for t, u in taps:
            put(t, u, block)
        flipped = block.T
        for t, u in taps:
            put(u, t, flipped)

    for a in range(3):
        line = {}
        for dc in range(3):
            line[dc] = x0[dc] - row1[dc] if a == 0 else (x0[dc] - row0[dc] if a == 2 else x0[dc])
        for b in range(3):
            block = line[0]
            if b == 0:
                block = block - col1[0]
                if a == 0:
                    block = block + corner[3]
                if a == 2:
                    block = block + corner[1]
            if b == 2:
                block = block - col0[0]
                if a == 0:
                    block = block + corner[2]
                if a == 2:
                    block = block + corner[0]
            put(3 * a + b, 3 * a + b, block)
        put_all([(3 * a, 3 * a + 1), (3 * a + 1, 3 * a + 2)], line[1])
        put_all([(3 * a, 3 * a + 2)], line[2])
    for dr in (1, 2):
        starts = range(3 - dr)
        for b in range(3):
            block = down[dr, 0]
            if b == 0:
                block = block - col1[dr]
            if b == 2:
                block = block - col0[dr]
            put_all([(3 * a + b, 3 * (a + dr) + b) for a in starts], block)
        for dc in (-2, -1, 1, 2):
            taps = [(3 * a + b, 3 * (a + dr) + b + dc) for a in starts for b in range(3) if 0 <= b + dc < 3]
            put_all(taps, down[dr, dc])

    e, inv_a = normalized(m_ref[...])
    hi, lo = split(e)
    e_hi[...] = hi
    e_lo[...] = lo
    g, _ = load("gg")
    eg, inv_g = normalized(g)
    eg2 = dot3(eg, eg)
    pg = eg + dot3(eg, eg2) + eg2
    w0 = load("w0z")
    w1 = load("w1z")
    w2 = load("w2z")
    w = jnp.concatenate([w00, w0[0], w0[1], w10, w1[0], w1[1], w20, w2[0], w2[1]], axis=1)
    w = w + dot3(pg, w)
    v = w.T * (inv_a * inv_g * total_rows)

    def apply(v):
        vh, vl = split(v)
        both = jnp.dot(e_hi[...], jnp.concatenate([vh, vl], axis=1), preferred_element_type=F32)
        return both[:, 0:C] + (both[:, C:PAIR] + jnp.dot(e_lo[...], vh, preferred_element_type=F32))

    v = v + apply(v)
    v = v + apply(apply(v))
    out_ref[...] = v.T


def precondition(near, far, total_rows):
    n = TAPS * C
    return pl.pallas_call(
        functools.partial(final_kernel, float(total_rows)),
        out_shape=jax.ShapeDtypeStruct((C, n), F32),
        in_specs=[pl.BlockSpec(memory_space=pltpu.VMEM)] * 2,
        out_specs=pl.BlockSpec(memory_space=pltpu.VMEM),
        scratch_shapes=[
            pltpu.VMEM((4, QUART, C, PAIR), F32),
            pltpu.VMEM((n, n), F32),
            pltpu.VMEM((n, n), BF16),
            pltpu.VMEM((n, n), BF16),
        ],
        compiler_params=pltpu.CompilerParams(vmem_limit_bytes=VMEM_LIMIT),
    )(near, far)


def pairings(n_dp, n_grp):
    n = n_dp * n_grp
    core_bit = n_grp
    first, second = 1, 2 * n_grp
    doublings = []
    bit = 4 * n_grp
    while bit < n:
        doublings.append(bit)
        bit *= 2
    orders = ([first, second] + doublings, [second, first] + doublings[::-1])
    pairs = lambda masks: [(i, i ^ masks[1 if i & core_bit else 0]) for i in range(n)]
    rounds = [pairs(masks) for masks in zip(*orders)]
    return pairs((core_bit, core_bit)), rounds[:2], rounds[2:], (pairs((first, first)), pairs((second, second)))


def shards(feature_maps, output_grads):
    n_dp, n_grp = lax.axis_size("dp"), lax.axis_size("grp")
    cores, halvings, doublings, gathers = pairings(n_dp, n_grp)
    swap = lambda a, p: lax.ppermute(a, ("dp", "grp"), p)
    total_rows = feature_maps.shape[2] * feature_maps.shape[3] // C * feature_maps.shape[1] * n_dp * n_grp
    got = swap(local_sums(feature_maps, output_grads, False), cores)
    keep = local_sums(feature_maps, output_grads, True)
    got_far = swap(keep[2:4] + got[2:4], halvings[0])
    got_next = swap(keep[1] + got[1] + got_far[1], halvings[1])
    own = keep[0] + got[0] + got_far[0] + got_next
    for p in doublings:
        own = own + swap(own, p)
    near = jnp.stack([own, swap(own, gathers[0])])
    far = swap(near, gathers[1])
    mine = precondition(near, far, total_rows)
    other = swap(mine, cores)
    core = lax.rem(lax.axis_index("dp"), 2)
    return jnp.where(core == 0, jnp.stack([mine, other]), jnp.stack([other, mine]))


def solution(mesh):
    placed = (P(None, ("dp", "grp"), None, None), P(None, ("dp", "grp"), None, None))
    return jax.shard_map(shards, mesh=mesh, in_specs=placed, out_specs=P(), check_vma=False)
```

```python
import functools

import jax
import jax.numpy as jnp
import numpy as np
from jax import lax
from jax.experimental import pallas as pl
from jax.experimental.pallas import tpu as pltpu
from jax.sharding import PartitionSpec as P

C = 64
TAPS = 9
PAIR = 2 * C
ROW = 64
QUART = 5
DAMP = 0.1
SUMS_VMEM = 53 * 2**20
VMEM_LIMIT = 48 * 2**20
F32 = jnp.float32
BF16 = jnp.bfloat16

PAIRS = (
    "x1m", "x1z", "cc1", "x2m", "x2z",
    "cc2", "x22", "x0z", "cc0", "r0z",
    "r1z", "k0", "k1", "w0z", "w1z",
    "w2z", "h0", "h1", "h2", "gg",
)
PLACE = {name: index for index, name in enumerate(PAIRS)}


def contract0(a, b):
    return lax.dot_general(a, b, (((0,), (0,)), ((), ())), preferred_element_type=F32)


def chip_place():
    dp = lax.axis_index("dp")
    core = lax.rem(dp, 2)
    second = lax.rem(dp // 2, 2)
    first = lax.axis_index("grp")
    return core, first, second


def slot_of(quarter, layer, first, second):
    mine_first = first ^ (quarter // 2)
    mine_second = second ^ (quarter % 2)
    major = jnp.where(layer == 0, mine_first, mine_second)
    minor = jnp.where(layer == 0, mine_second, mine_first)
    return 2 * major + minor


def gathered_slot(quarter, first, second):
    return 2 * (second ^ (quarter % 2)) + (first ^ (quarter // 2))


def local_kernel(height, width, own, x_hbm, g_hbm, out_ref, xbuf, gbuf, shifted, lhs_t, edges, sems):
    core, first, second = chip_place()
    wp = width // 2
    rows = wp * ROW
    layer = core if own else 1 - core
    copy_x = pltpu.make_async_copy(x_hbm.at[layer, 0], xbuf, sems.at[0])
    copy_g = pltpu.make_async_copy(g_hbm.at[layer, 0], gbuf, sems.at[1])
    copy_x.start()
    copy_g.start()
    for d in range(4):
        shifted[d, 0:ROW, :] = jnp.zeros((ROW, PAIR), BF16)
        shifted[d, ROW + rows : 2 * ROW + rows, :] = jnp.zeros((ROW, PAIR), BF16)
    edges[...] = jnp.zeros_like(edges)
    low = lax.broadcasted_iota(jnp.int32, (ROW, PAIR), 1) < C
    pad = jnp.zeros((ROW - height, PAIR), F32)
    n_edge = edges.shape[1] - 16
    copy_x.wait()
    copy_g.wait()
    for pair in range(wp // 2):
        tiles_x = []
        tiles_g = []
        for half in range(2):
            j = 2 * pair + half
            block = jnp.concatenate([xbuf[:, j * PAIR : (j + 1) * PAIR].astype(F32), pad], axis=0)
            at = ROW + j * ROW
            edges[0, 8 + j : 9 + j, :] = block[0:1, :]
            edges[1, 8 + j : 9 + j, :] = block[height - 1 : height, :]
            shifted[0, at : at + ROW, :] = pltpu.roll(block, 1, 0).astype(BF16)
            shifted[1, at : at + ROW, :] = block.astype(BF16)
            shifted[2, at : at + ROW, :] = pltpu.roll(block, ROW - 1, 0).astype(BF16)
            shifted[3, at : at + ROW, :] = pltpu.roll(block, ROW - 2, 0).astype(BF16)
            tiles_x.append(block)
            tiles_g.append(jnp.concatenate([gbuf[:, j * PAIR : (j + 1) * PAIR].astype(F32), pad], axis=0))
        lanes = slice(pair * PAIR, (pair + 1) * PAIR)
        lhs_t[0:PAIR, lanes] = jnp.concatenate(tiles_x, axis=0).T.astype(BF16)
        lhs_t[PAIR : 2 * PAIR, lanes] = jnp.concatenate(tiles_g, axis=0).T.astype(BF16)

    def product(d, s, part):
        left = lhs_t[...] if part is None else lhs_t[part * PAIR : (part + 1) * PAIR, :]
        right = [shifted[d, (1 + one) * ROW : (1 + one) * ROW + rows, :] for one in s]
        right = right[0] if len(right) == 1 else jnp.concatenate(right, axis=1)
        full = jnp.dot(left, right, preferred_element_type=F32)
        return [full[:, k * PAIR : (k + 1) * PAIR] for k in range(len(s))]

    def table(at_s, base, s):
        upper = at_s[s][base : base + C, :]
        here = pltpu.roll(at_s[s][base + C : base + PAIR, :], C, 1)
        if s + 1 not in at_s:
            return upper + here
        after = pltpu.roll(at_s[s + 1][base + C : base + PAIR, :], C, 1)
        return upper + jnp.where(low, here, after)

    def odd(at_s, base, s):
        return at_s[s][base : base + C, :] + pltpu.roll(at_s[s + 1][base + C : base + PAIR, :], C, 1)

    def store(name, value):
        index = PLACE[name]
        slot = slot_of(index // QUART, layer, first, second)
        out_ref[slot, index % QUART] = value

    p = product(0, (-1, 0), 1) + product(0, (1,), 1)
    at_s = dict(zip((-1, 0, 1), p))
    store("w0z", table(at_s, 0, 0))
    w0 = odd(at_s, 0, -1)
    p = product(1, (-1, 0), None) + product(1, (1,), None)
    at_s = dict(zip((-1, 0, 1), p))
    store("x0z", table(at_s, 0, 0))
    store("h0", jnp.where(low, table(at_s, 0, 1), w0))
    store("w1z", table(at_s, PAIR, 0))
    w1 = odd(at_s, PAIR, -1)
    p = product(2, (-1, 0), None) + product(2, (1,), None)
    at_s = dict(zip((-1, 0, 1), p))
    store("x1m", table(at_s, 0, -1))
    store("x1z", table(at_s, 0, 0))
    x12 = table(at_s, 0, 1)
    store("w2z", table(at_s, PAIR, 0))
    w2 = odd(at_s, PAIR, -1)
    p = product(3, (-1, 0), 0) + product(3, (1,), 0)
    at_s = dict(zip((-1, 0, 1), p))
    store("x2m", table(at_s, 0, -1))
    store("x2z", table(at_s, 0, 0))
    store("x22", jnp.where(low, x12, pltpu.roll(table(at_s, 0, 1), C, 1)))
    gl = lhs_t[PAIR : 2 * PAIR, :]
    gg = lax.dot_general(gl, gl, (((1,), (1,)), ((), ())), preferred_element_type=F32)
    store("gg", gg[0:C, :] + pltpu.roll(gg[C:PAIR, :], C, 1))
    fl = [
        jnp.where(
            low,
            shifted[d, ROW : 2 * ROW, :].astype(F32),
            shifted[d, rows : ROW + rows, :].astype(F32),
        ).astype(BF16)
        for d in (1, 2, 3)
    ]
    for d, name in enumerate(("cc0", "cc1", "cc2")):
        q = contract0(fl[0], fl[d])
        store(name, jnp.where(low, q[0:C, :], q[C:PAIR, :]))
    line = lax.broadcasted_iota(jnp.int32, (n_edge, PAIR), 0)
    lane = lax.broadcasted_iota(jnp.int32, (n_edge, PAIR), 1)
    corner = ((line == 0) & (lane < C)) | ((line == wp - 1) & (lane >= C))
    halves = []
    for e in range(2):
        zero = edges[e, 8 : 8 + n_edge, :]
        here = zero.astype(BF16)
        after = edges[e, 9 : 9 + n_edge, :].astype(BF16)
        at_s = {0: contract0(here, here), 1: contract0(here, after)}
        store(("r0z", "r1z")[e], table(at_s, 0, 0))
        halves.append(table(at_s, 0, 1))
        only = jnp.where(corner, zero, 0.0).astype(BF16)
        q = contract0(only, only)
        store(("k0", "k1")[e], jnp.where(low, q[0:C, :], q[C:PAIR, :]))
    store("h1", jnp.where(low, halves[0], w1))
    store("h2", jnp.where(low, halves[1], w2))


def local_sums(feature_maps, output_grads, own):
    height = feature_maps.shape[2]
    width = feature_maps.shape[3] // C
    wp = width // 2
    shape = jax.ShapeDtypeStruct((4, QUART, C, PAIR), F32)
    n_edge = (wp + 15) // 16 * 16
    return pl.pallas_call(
        functools.partial(local_kernel, height, width, own),
        out_shape=shape,
        in_specs=[pl.BlockSpec(memory_space=pltpu.HBM)] * 2,
        out_specs=pl.BlockSpec(memory_space=pltpu.VMEM),
        scratch_shapes=[
            pltpu.VMEM((height, width * C), BF16),
            pltpu.VMEM((height, width * C), BF16),
            pltpu.VMEM((4, (wp + 2) * ROW, PAIR), BF16),
            pltpu.VMEM((2 * PAIR, wp * ROW), BF16),
            pltpu.VMEM((2, n_edge + 16, PAIR), F32),
            pltpu.SemaphoreType.DMA((2,)),
        ],
        compiler_params=pltpu.CompilerParams(vmem_limit_bytes=SUMS_VMEM),
    )(feature_maps, output_grads)


def split(a):
    high = a.astype(BF16)
    return high, (a - high.astype(F32)).astype(BF16)


def dot3(a, b):
    ah, al = split(a)
    bh, bl = split(b)
    dot = functools.partial(jnp.dot, preferred_element_type=F32)
    return dot(ah, bh) + (dot(ah, bl) + dot(al, bh))


def normalized(m):
    n = m.shape[0]
    diag = lax.broadcasted_iota(jnp.int32, (n, n), 0) == lax.broadcasted_iota(jnp.int32, (n, n), 1)
    trace = jnp.sum(jnp.where(diag, m, 0.0))
    m = m + jnp.where(diag, DAMP * trace / n, 0.0)
    inv = lax.rsqrt(jnp.sum(m * m))
    return jnp.where(diag, 1.0, 0.0) - m * inv, inv


def final_kernel(total_rows, own_ref, beside_ref, below_ref, across_ref, out_ref, quarters, m_ref, e_hi, e_lo):
    _, first, second = chip_place()
    for slot, ref in enumerate((own_ref, beside_ref, below_ref, across_ref)):
        quarters[slot] = ref[...]

    def load(name):
        index = PLACE[name]
        both = quarters[gathered_slot(index // QUART, first, second), index % QUART]
        return both[:, 0:C], both[:, C:PAIR]

    x0 = dict(zip((0, 1), load("x0z")))
    h0, w00 = load("h0")
    x0[2] = h0
    row0 = dict(zip((0, 1), load("r0z")))
    row0[2], w10 = load("h1")
    row1 = dict(zip((0, 1), load("r1z")))
    row1[2], w20 = load("h2")
    col0 = {}
    col1 = {}
    col0[0], col1[0] = load("cc0")
    corner = load("k0") + load("k1")
    down = {}
    for dr in (1, 2):
        down[dr, -2], down[dr, -1] = load("x%dm" % dr)
        down[dr, 0], down[dr, 1] = load("x%dz" % dr)
        col0[dr], col1[dr] = load("cc%d" % dr)
    down[1, 2], down[2, 2] = load("x22")

    def put(t, u, block):
        m_ref[t * C : (t + 1) * C, u * C : (u + 1) * C] = block

    def put_all(taps, block):
        for t, u in taps:
            put(t, u, block)
        flipped = block.T
        for t, u in taps:
            put(u, t, flipped)

    for a in range(3):
        line = {}
        for dc in range(3):
            line[dc] = x0[dc] - row1[dc] if a == 0 else (x0[dc] - row0[dc] if a == 2 else x0[dc])
        for b in range(3):
            block = line[0]
            if b == 0:
                block = block - col1[0]
                if a == 0:
                    block = block + corner[3]
                if a == 2:
                    block = block + corner[1]
            if b == 2:
                block = block - col0[0]
                if a == 0:
                    block = block + corner[2]
                if a == 2:
                    block = block + corner[0]
            put(3 * a + b, 3 * a + b, block)
        put_all([(3 * a, 3 * a + 1), (3 * a + 1, 3 * a + 2)], line[1])
        put_all([(3 * a, 3 * a + 2)], line[2])
    for dr in (1, 2):
        starts = range(3 - dr)
        for b in range(3):
            block = down[dr, 0]
            if b == 0:
                block = block - col1[dr]
            if b == 2:
                block = block - col0[dr]
            put_all([(3 * a + b, 3 * (a + dr) + b) for a in starts], block)
        for dc in (-2, -1, 1, 2):
            taps = [(3 * a + b, 3 * (a + dr) + b + dc) for a in starts for b in range(3) if 0 <= b + dc < 3]
            put_all(taps, down[dr, dc])

    e, inv_a = normalized(m_ref[...])
    hi, lo = split(e)
    e_hi[...] = hi
    e_lo[...] = lo
    g, _ = load("gg")
    eg, inv_g = normalized(g)
    eg2 = dot3(eg, eg)
    pg = eg + dot3(eg, eg2) + eg2
    w0 = load("w0z")
    w1 = load("w1z")
    w2 = load("w2z")
    w = jnp.concatenate([w00, w0[0], w0[1], w10, w1[0], w1[1], w20, w2[0], w2[1]], axis=1)
    w = w + dot3(pg, w)
    v = w.T * (inv_a * inv_g * total_rows)

    def apply(v):
        vh, vl = split(v)
        both = jnp.dot(e_hi[...], jnp.concatenate([vh, vl], axis=1), preferred_element_type=F32)
        return both[:, 0:C] + (both[:, C:PAIR] + jnp.dot(e_lo[...], vh, preferred_element_type=F32))

    v = v + apply(v)
    v = v + apply(apply(v))
    out_ref[...] = v.T


def precondition(parts, total_rows):
    n = TAPS * C
    return pl.pallas_call(
        functools.partial(final_kernel, float(total_rows)),
        out_shape=jax.ShapeDtypeStruct((C, n), F32),
        in_specs=[pl.BlockSpec(memory_space=pltpu.VMEM)] * 4,
        out_specs=pl.BlockSpec(memory_space=pltpu.VMEM),
        scratch_shapes=[
            pltpu.VMEM((4, QUART, C, PAIR), F32),
            pltpu.VMEM((n, n), F32),
            pltpu.VMEM((n, n), BF16),
            pltpu.VMEM((n, n), BF16),
        ],
        compiler_params=pltpu.CompilerParams(vmem_limit_bytes=VMEM_LIMIT),
    )(*parts)


def pairings(n_dp, n_grp):
    n = n_dp * n_grp
    core_bit = n_grp
    first, second = 1, 2 * n_grp
    doublings = []
    bit = 4 * n_grp
    while bit < n:
        doublings.append(bit)
        bit *= 2
    orders = ([first, second] + doublings, [second, first] + doublings[::-1])
    pairs = lambda masks: [(i, i ^ masks[1 if i & core_bit else 0]) for i in range(n)]
    rounds = [pairs(masks) for masks in zip(*orders)]
    return pairs((core_bit, core_bit)), rounds[:2], rounds[2:], (pairs((first, first)), pairs((second, second)))


def shards(feature_maps, output_grads):
    n_dp, n_grp = lax.axis_size("dp"), lax.axis_size("grp")
    cores, halvings, doublings, gathers = pairings(n_dp, n_grp)
    swap = lambda a, p: lax.ppermute(a, ("dp", "grp"), p)
    total_rows = feature_maps.shape[2] * feature_maps.shape[3] // C * feature_maps.shape[1] * n_dp * n_grp
    got = swap(local_sums(feature_maps, output_grads, False), cores)
    keep = local_sums(feature_maps, output_grads, True)
    far_next = swap(keep[3] + got[3], halvings[0])
    far_own = swap(keep[2] + got[2], halvings[0])
    got_next = swap(keep[1] + got[1] + far_next, halvings[1])
    own = keep[0] + got[0] + far_own + got_next
    for p in doublings:
        own = own + swap(own, p)
    beside = swap(own, gathers[0])
    below = swap(own, gathers[1])
    across = swap(beside, gathers[1])
    mine = precondition((own, beside, below, across), total_rows)
    other = swap(mine, cores)
    core = lax.rem(lax.axis_index("dp"), 2)
    return jnp.where(core == 0, jnp.stack([mine, other]), jnp.stack([other, mine]))


def solution(mesh):
    placed = (P(None, ("dp", "grp"), None, None), P(None, ("dp", "grp"), None, None))
    return jax.shard_map(shards, mesh=mesh, in_specs=placed, out_specs=P(), check_vma=False)
```

```python
import functools

import jax
import jax.numpy as jnp
import numpy as np
from jax import lax
from jax.experimental import pallas as pl
from jax.experimental.pallas import tpu as pltpu
from jax.sharding import PartitionSpec as P

C = 64
TAPS = 9
PAIR = 2 * C
ROW = 64
QUART = 4
DAMP = 0.1
SUMS_VMEM = 53 * 2**20
VMEM_LIMIT = 48 * 2**20
F32 = jnp.float32
BF16 = jnp.bfloat16

PAIRS = (
    "x1m", "x1z", "cc1", "x2m",
    "x2z", "cc2", "x22", "kk",
    "cg", "w0z", "w1z", "w2z",
    "h0", "h1", "h2", "r01",
)
PLACE = {name: index for index, name in enumerate(PAIRS)}
LAST = QUART * ROW
PIECE = ROW // 4
DIAGS = LAST + PIECE
QROWS = DIAGS + 8


def contract0(a, b):
    return lax.dot_general(a, b, (((0,), (0,)), ((), ())), preferred_element_type=F32)


def chip_place():
    dp = lax.axis_index("dp")
    core = lax.rem(dp, 2)
    second = lax.rem(dp // 2, 2)
    first = lax.axis_index("grp")
    return core, first, second


def slot_of(quarter, layer, first, second):
    mine_first = first ^ (quarter // 2)
    mine_second = second ^ (quarter % 2)
    major = jnp.where(layer == 0, mine_first, mine_second)
    minor = jnp.where(layer == 0, mine_second, mine_first)
    return 2 * major + minor


def gathered_slot(quarter, first, second):
    return 2 * (second ^ (quarter % 2)) + (first ^ (quarter // 2))


def local_kernel(height, width, own, x_hbm, g_hbm, out_ref, xbuf, gbuf, shifted, lhs_t, edges, sems):
    core, first, second = chip_place()
    wp = width // 2
    rows = wp * ROW
    layer = core if own else 1 - core
    copy_x = pltpu.make_async_copy(x_hbm.at[layer, 0], xbuf, sems.at[0])
    copy_g = pltpu.make_async_copy(g_hbm.at[layer, 0], gbuf, sems.at[1])
    copy_x.start()
    copy_g.start()
    for d in range(4):
        shifted[d, 0:ROW, :] = jnp.zeros((ROW, PAIR), BF16)
        shifted[d, ROW + rows : 2 * ROW + rows, :] = jnp.zeros((ROW, PAIR), BF16)
    edges[...] = jnp.zeros_like(edges)
    low = lax.broadcasted_iota(jnp.int32, (ROW, PAIR), 1) < C
    pad = jnp.zeros((ROW - height, PAIR), F32)
    n_edge = edges.shape[1] - 16
    copy_x.wait()
    copy_g.wait()
    for pair in range(wp // 2):
        tiles_x = []
        tiles_g = []
        for half in range(2):
            j = 2 * pair + half
            block = jnp.concatenate([xbuf[:, j * PAIR : (j + 1) * PAIR].astype(F32), pad], axis=0)
            at = ROW + j * ROW
            edges[0, 8 + j : 9 + j, :] = block[0:1, :]
            edges[1, 8 + j : 9 + j, :] = block[height - 1 : height, :]
            shifted[0, at : at + ROW, :] = pltpu.roll(block, 1, 0).astype(BF16)
            shifted[1, at : at + ROW, :] = block.astype(BF16)
            shifted[2, at : at + ROW, :] = pltpu.roll(block, ROW - 1, 0).astype(BF16)
            shifted[3, at : at + ROW, :] = pltpu.roll(block, ROW - 2, 0).astype(BF16)
            tiles_x.append(block)
            tiles_g.append(jnp.concatenate([gbuf[:, j * PAIR : (j + 1) * PAIR].astype(F32), pad], axis=0))
        lanes = slice(pair * PAIR, (pair + 1) * PAIR)
        lhs_t[0:PAIR, lanes] = jnp.concatenate(tiles_x, axis=0).T.astype(BF16)
        lhs_t[PAIR : 2 * PAIR, lanes] = jnp.concatenate(tiles_g, axis=0).T.astype(BF16)

    def product(d, s, part):
        left = lhs_t[...] if part is None else lhs_t[part * PAIR : (part + 1) * PAIR, :]
        right = [shifted[d, (1 + one) * ROW : (1 + one) * ROW + rows, :] for one in s]
        right = right[0] if len(right) == 1 else jnp.concatenate(right, axis=1)
        full = jnp.dot(left, right, preferred_element_type=F32)
        return [full[:, k * PAIR : (k + 1) * PAIR] for k in range(len(s))]

    def table(at_s, base, s):
        upper = at_s[s][base : base + C, :]
        here = pltpu.roll(at_s[s][base + C : base + PAIR, :], C, 1)
        if s + 1 not in at_s:
            return upper + here
        after = pltpu.roll(at_s[s + 1][base + C : base + PAIR, :], C, 1)
        return upper + jnp.where(low, here, after)

    def odd(at_s, base, s):
        return at_s[s][base : base + C, :] + pltpu.roll(at_s[s + 1][base + C : base + PAIR, :], C, 1)

    def store(name, value):
        index = PLACE[name]
        slot = slot_of(index // QUART, layer, first, second)
        at = index % QUART * ROW
        out_ref[slot, at : at + ROW, :] = value

    row = lax.broadcasted_iota(jnp.int32, (ROW, PAIR), 0)
    col = lax.rem(lax.broadcasted_iota(jnp.int32, (ROW, PAIR), 1), C)
    pack = lambda a, b: jnp.where(row >= col, a, b)
    diagonal = lambda a: jnp.sum(jnp.where(row == col, a, 0.0), axis=0, keepdims=True)

    p = product(0, (-1, 0), 1) + product(0, (1,), 1)
    at_s = dict(zip((-1, 0, 1), p))
    store("w0z", table(at_s, 0, 0))
    w0 = odd(at_s, 0, -1)
    p = product(1, (-1, 0), None) + product(1, (1,), None)
    at_s = dict(zip((-1, 0, 1), p))
    x0z = table(at_s, 0, 0)
    store("h0", jnp.where(low, table(at_s, 0, 1), w0))
    store("w1z", table(at_s, PAIR, 0))
    w1 = odd(at_s, PAIR, -1)
    p = product(2, (-1, 0), None) + product(2, (1,), None)
    at_s = dict(zip((-1, 0, 1), p))
    store("x1m", table(at_s, 0, -1))
    store("x1z", table(at_s, 0, 0))
    x12 = table(at_s, 0, 1)
    store("w2z", table(at_s, PAIR, 0))
    w2 = odd(at_s, PAIR, -1)
    p = product(3, (-1, 0), 0) + product(3, (1,), 0)
    at_s = dict(zip((-1, 0, 1), p))
    store("x2m", table(at_s, 0, -1))
    store("x2z", table(at_s, 0, 0))
    store("x22", jnp.where(low, x12, pltpu.roll(table(at_s, 0, 1), C, 1)))
    gl = lhs_t[PAIR : 2 * PAIR, :]
    gg = lax.dot_general(gl, gl, (((1,), (1,)), ((), ())), preferred_element_type=F32)
    gx = jnp.where(low, gg[0:C, :] + pltpu.roll(gg[C:PAIR, :], C, 1), pltpu.roll(x0z, C, 1))
    fl = [
        jnp.where(
            low,
            shifted[d, ROW : 2 * ROW, :].astype(F32),
            shifted[d, rows : ROW + rows, :].astype(F32),
        ).astype(BF16)
        for d in (1, 2, 3)
    ]
    for d, name in enumerate(("cg", "cc1", "cc2")):
        q = contract0(fl[0], fl[d])
        both = jnp.where(low, q[0:C, :], q[C:PAIR, :])
        if d == 0:
            name, both = "cg", pack(both, gx)
        store(name, both)
    line = lax.broadcasted_iota(jnp.int32, (n_edge, PAIR), 0)
    lane = lax.broadcasted_iota(jnp.int32, (n_edge, PAIR), 1)
    corner = ((line == 0) & (lane < C)) | ((line == wp - 1) & (lane >= C))
    halves = []
    lines = []
    corners = []
    for e in range(2):
        zero = edges[e, 8 : 8 + n_edge, :]
        here = zero.astype(BF16)
        after = edges[e, 9 : 9 + n_edge, :].astype(BF16)
        at_s = {0: contract0(here, here), 1: contract0(here, after)}
        lines.append(table(at_s, 0, 0))
        halves.append(table(at_s, 0, 1))
        only = jnp.where(corner, zero, 0.0).astype(BF16)
        q = contract0(only, only)
        corners.append(jnp.where(low, q[0:C, :], q[C:PAIR, :]))
    store("h1", jnp.where(low, halves[0], w1))
    store("h2", jnp.where(low, halves[1], w2))
    store("kk", pack(corners[0], corners[1]))
    store("r01", jnp.where(low, pltpu.roll(lines[0], C, 1), lines[1]))
    rx = jnp.where(low, pack(lines[0], lines[1]), x0z)
    diags = jnp.concatenate(
        [diagonal(corners[1]), diagonal(gx), diagonal(lines[1]), jnp.zeros((5, PAIR), F32)], axis=0
    )
    for quarter in range(4):
        slot = slot_of(quarter, layer, first, second)
        out_ref[slot, LAST:DIAGS, :] = rx[quarter * PIECE : (quarter + 1) * PIECE, :]
        out_ref[slot, DIAGS:QROWS, :] = diags


def local_sums(feature_maps, output_grads, own):
    height = feature_maps.shape[2]
    width = feature_maps.shape[3] // C
    wp = width // 2
    shape = jax.ShapeDtypeStruct((4, QROWS, PAIR), F32)
    n_edge = (wp + 15) // 16 * 16
    return pl.pallas_call(
        functools.partial(local_kernel, height, width, own),
        out_shape=shape,
        in_specs=[pl.BlockSpec(memory_space=pltpu.HBM)] * 2,
        out_specs=pl.BlockSpec(memory_space=pltpu.VMEM),
        scratch_shapes=[
            pltpu.VMEM((height, width * C), BF16),
            pltpu.VMEM((height, width * C), BF16),
            pltpu.VMEM((4, (wp + 2) * ROW, PAIR), BF16),
            pltpu.VMEM((2 * PAIR, wp * ROW), BF16),
            pltpu.VMEM((2, n_edge + 16, PAIR), F32),
            pltpu.SemaphoreType.DMA((2,)),
        ],
        compiler_params=pltpu.CompilerParams(vmem_limit_bytes=SUMS_VMEM),
    )(feature_maps, output_grads)


def split(a):
    high = a.astype(BF16)
    return high, (a - high.astype(F32)).astype(BF16)


def dot3(a, b):
    ah, al = split(a)
    bh, bl = split(b)
    dot = functools.partial(jnp.dot, preferred_element_type=F32)
    return dot(ah, bh) + (dot(ah, bl) + dot(al, bh))


def normalized(m):
    n = m.shape[0]
    diag = lax.broadcasted_iota(jnp.int32, (n, n), 0) == lax.broadcasted_iota(jnp.int32, (n, n), 1)
    trace = jnp.sum(jnp.where(diag, m, 0.0))
    m = m + jnp.where(diag, DAMP * trace / n, 0.0)
    inv = lax.rsqrt(jnp.sum(m * m))
    return jnp.where(diag, 1.0, 0.0) - m * inv, inv


def final_kernel(total_rows, own_ref, beside_ref, below_ref, across_ref, out_ref, quarters, m_hi, m_lo):
    _, first, second = chip_place()
    for slot, ref in enumerate((own_ref, beside_ref, below_ref, across_ref)):
        quarters[slot] = ref[...]

    def slot(quarter):
        return gathered_slot(quarter, first, second)

    def load(name):
        index = PLACE[name]
        at = index % QUART * ROW
        both = quarters[slot(index // QUART), at : at + ROW, :]
        return both[:, 0:C], both[:, C:PAIR]

    row = lax.broadcasted_iota(jnp.int32, (C, C), 0)
    col = lax.broadcasted_iota(jnp.int32, (C, C), 1)
    diags = quarters[slot(0), DIAGS:QROWS, :]

    def unpack(block, line, at):
        flipped = block.T
        mirrored = jnp.where(row < col, block, flipped)
        diagonal = jnp.broadcast_to(diags[line : line + 1, at : at + C], (C, C))
        return jnp.where(row >= col, block, flipped), jnp.where(row == col, diagonal, mirrored)

    rx = jnp.concatenate([quarters[slot(quarter), LAST:DIAGS, :] for quarter in range(4)], axis=0)
    x0 = {1: rx[:, C:PAIR]}
    row0 = {}
    row1 = {}
    col0 = {}
    col1 = {}
    row0[0], row1[0] = unpack(rx[:, 0:C], 2, 0)
    row0[1], row1[1] = load("r01")
    x0[2], w00 = load("h0")
    row0[2], w10 = load("h1")
    row1[2], w20 = load("h2")
    low, high = load("cg")
    col0[0], g = unpack(low, 1, 0)
    col1[0], x0[0] = unpack(high, 1, C)
    low, high = load("kk")
    k00, k10 = unpack(low, 0, 0)
    k01, k11 = unpack(high, 0, C)
    corner = (k00, k01, k10, k11)
    down = {}
    for dr in (1, 2):
        down[dr, -2], down[dr, -1] = load("x%dm" % dr)
        down[dr, 0], down[dr, 1] = load("x%dz" % dr)
        col0[dr], col1[dr] = load("cc%d" % dr)
    down[1, 2], down[2, 2] = load("x22")

    squares = []

    def put(t, u, block):
        high, rest = split(block)
        m_hi[t * C : (t + 1) * C, u * C : (u + 1) * C] = high
        m_lo[t * C : (t + 1) * C, u * C : (u + 1) * C] = rest

    def put_all(taps, block):
        squares.append(2.0 * len(taps) * (block * block))
        for t, u in taps:
            put(t, u, block)
        flipped = block.T
        for t, u in taps:
            put(u, t, flipped)

    on_diagonal = []
    for a in range(3):
        line = {}
        for dc in range(3):
            line[dc] = x0[dc] - row1[dc] if a == 0 else (x0[dc] - row0[dc] if a == 2 else x0[dc])
        for b in range(3):
            block = line[0]
            if b == 0:
                block = block - col1[0]
                if a == 0:
                    block = block + corner[3]
                if a == 2:
                    block = block + corner[1]
            if b == 2:
                block = block - col0[0]
                if a == 0:
                    block = block + corner[2]
                if a == 2:
                    block = block + corner[0]
            squares.append(block * block)
            on_diagonal.append(block)
            put(3 * a + b, 3 * a + b, block)
        put_all([(3 * a, 3 * a + 1), (3 * a + 1, 3 * a + 2)], line[1])
        put_all([(3 * a, 3 * a + 2)], line[2])
    for dr in (1, 2):
        starts = range(3 - dr)
        for b in range(3):
            block = down[dr, 0]
            if b == 0:
                block = block - col1[dr]
            if b == 2:
                block = block - col0[dr]
            put_all([(3 * a + b, 3 * (a + dr) + b) for a in starts], block)
        for dc in (-2, -1, 1, 2):
            taps = [(3 * a + b, 3 * (a + dr) + b + dc) for a in starts for b in range(3) if 0 <= b + dc < 3]
            put_all(taps, down[dr, dc])

    n = TAPS * C
    trace = jnp.sum(jnp.where(row == col, sum(on_diagonal), 0.0))
    shift = DAMP * trace / n
    inv_a = lax.rsqrt(jnp.sum(sum(squares)) + shift * (2.0 * trace + n * shift))
    keep = 1.0 - inv_a * shift
    eg, inv_g = normalized(g)
    eg2 = dot3(eg, eg)
    pg = eg + dot3(eg, eg2) + eg2
    w0 = load("w0z")
    w1 = load("w1z")
    w2 = load("w2z")
    w = jnp.concatenate([w00, w0[0], w0[1], w10, w1[0], w1[1], w20, w2[0], w2[1]], axis=1)
    w = w + dot3(pg, w)
    v = w.T * (inv_a * inv_g * total_rows)

    def apply(v):
        vh, vl = split(v)
        both = jnp.dot(m_hi[...], jnp.concatenate([vh, vl], axis=1), preferred_element_type=F32)
        mv = both[:, 0:C] + (both[:, C:PAIR] + jnp.dot(m_lo[...], vh, preferred_element_type=F32))
        return keep * v - inv_a * mv

    v = v + apply(v)
    v = v + apply(apply(v))
    out_ref[...] = v.T


def precondition(parts, total_rows):
    n = TAPS * C
    return pl.pallas_call(
        functools.partial(final_kernel, float(total_rows)),
        out_shape=jax.ShapeDtypeStruct((C, n), F32),
        in_specs=[pl.BlockSpec(memory_space=pltpu.VMEM)] * 4,
        out_specs=pl.BlockSpec(memory_space=pltpu.VMEM),
        scratch_shapes=[
            pltpu.VMEM((4, QROWS, PAIR), F32),
            pltpu.VMEM((n, n), BF16),
            pltpu.VMEM((n, n), BF16),
        ],
        compiler_params=pltpu.CompilerParams(vmem_limit_bytes=VMEM_LIMIT),
    )(*parts)


def pairings(n_dp, n_grp):
    n = n_dp * n_grp
    core_bit = n_grp
    first, second = 1, 2 * n_grp
    doublings = []
    bit = 4 * n_grp
    while bit < n:
        doublings.append(bit)
        bit *= 2
    orders = ([first, second] + doublings, [second, first] + doublings[::-1])
    pairs = lambda masks: [(i, i ^ masks[1 if i & core_bit else 0]) for i in range(n)]
    rounds = [pairs(masks) for masks in zip(*orders)]
    return pairs((core_bit, core_bit)), rounds[:2], rounds[2:], (pairs((first, first)), pairs((second, second)), pairs((first + second, first + second)))


def shards(feature_maps, output_grads):
    n_dp, n_grp = lax.axis_size("dp"), lax.axis_size("grp")
    cores, halvings, doublings, gathers = pairings(n_dp, n_grp)
    swap = lambda a, p: lax.ppermute(a, ("dp", "grp"), p)
    total_rows = feature_maps.shape[2] * feature_maps.shape[3] // C * feature_maps.shape[1] * n_dp * n_grp
    got = swap(local_sums(feature_maps, output_grads, False), cores)
    keep = local_sums(feature_maps, output_grads, True)
    far_next = swap(keep[3] + got[3], halvings[0])
    far_own = swap(keep[2] + got[2], halvings[0])
    got_next = swap(keep[1] + got[1] + far_next, halvings[1])
    own = keep[0] + got[0] + far_own + got_next
    for p in doublings:
        own = own + swap(own, p)
    beside = swap(own, gathers[0])
    below = swap(own, gathers[1])
    across = swap(own, gathers[2])
    mine = precondition((own, beside, below, across), total_rows)
    other = swap(mine, cores)
    core = lax.rem(lax.axis_index("dp"), 2)
    return jnp.where(core == 0, jnp.stack([mine, other]), jnp.stack([other, mine]))


def solution(mesh):
    placed = (P(None, ("dp", "grp"), None, None), P(None, ("dp", "grp"), None, None))
    return jax.shard_map(shards, mesh=mesh, in_specs=placed, out_specs=P(), check_vma=False)
```

```python
import functools

import jax
import jax.numpy as jnp
import numpy as np
from jax import lax
from jax.experimental import pallas as pl
from jax.experimental.pallas import tpu as pltpu
from jax.sharding import PartitionSpec as P

C = 64
TAPS = 9
PAIR = 2 * C
ROW = 64
QUART = 4
DAMP = 0.1
SUMS_VMEM = 52 * 2**20
VMEM_LIMIT = 48 * 2**20
F32 = jnp.float32
BF16 = jnp.bfloat16

PAIRS = (
    "x1m", "x1z", "cc1", "x2m",
    "x2z", "cc2", "x22", "kk",
    "cg", "w0z", "w1z", "w2z",
    "h0", "h1", "h2", "r01",
)
PLACE = {name: index for index, name in enumerate(PAIRS)}
LAST = QUART * ROW
PIECE = ROW // 4
DIAGS = LAST + PIECE
QROWS = DIAGS + 8


def contract0(a, b):
    return lax.dot_general(a, b, (((0,), (0,)), ((), ())), preferred_element_type=F32)


def chip_place():
    dp = lax.axis_index("dp")
    core = lax.rem(dp, 2)
    second = lax.rem(dp // 2, 2)
    first = lax.axis_index("grp")
    return core, first, second


def slot_of(quarter, layer, first, second):
    mine_first = first ^ (quarter // 2)
    mine_second = second ^ (quarter % 2)
    major = jnp.where(layer == 0, mine_first, mine_second)
    minor = jnp.where(layer == 0, mine_second, mine_first)
    return 2 * major + minor


def gathered_slot(quarter, first, second):
    return 2 * (second ^ (quarter % 2)) + (first ^ (quarter // 2))


def local_kernel(height, width, own, *refs):
    if own:
        xbuf, gbuf, out_ref, shifted, lhs_t, edges = refs
    else:
        x_hbm, g_hbm, out_ref, next_x, next_g, xbuf, gbuf, shifted, lhs_t, edges, sems = refs
    core, first, second = chip_place()
    wp = width // 2
    rows = wp * ROW
    layer = core if own else 1 - core
    if not own:
        copies = [
            pltpu.make_async_copy(x_hbm.at[layer, 0], xbuf, sems.at[0]),
            pltpu.make_async_copy(g_hbm.at[layer, 0], gbuf, sems.at[1]),
            pltpu.make_async_copy(x_hbm.at[core, 0], next_x, sems.at[2]),
            pltpu.make_async_copy(g_hbm.at[core, 0], next_g, sems.at[3]),
        ]
        for one in copies:
            one.start()
    for d in range(4):
        shifted[d, 0:ROW, :] = jnp.zeros((ROW, PAIR), BF16)
        shifted[d, ROW + rows : 2 * ROW + rows, :] = jnp.zeros((ROW, PAIR), BF16)
    edges[...] = jnp.zeros_like(edges)
    low = lax.broadcasted_iota(jnp.int32, (ROW, PAIR), 1) < C
    pad = jnp.zeros((ROW - height, PAIR), F32)
    n_edge = edges.shape[1] - 16
    if not own:
        copies[0].wait()
        copies[1].wait()
    for pair in range(wp // 2):
        tiles_x = []
        tiles_g = []
        for half in range(2):
            j = 2 * pair + half
            block = jnp.concatenate([xbuf[:, j * PAIR : (j + 1) * PAIR].astype(F32), pad], axis=0)
            at = ROW + j * ROW
            edges[0, 8 + j : 9 + j, :] = block[0:1, :]
            edges[1, 8 + j : 9 + j, :] = block[height - 1 : height, :]
            shifted[0, at : at + ROW, :] = pltpu.roll(block, 1, 0).astype(BF16)
            shifted[1, at : at + ROW, :] = block.astype(BF16)
            shifted[2, at : at + ROW, :] = pltpu.roll(block, ROW - 1, 0).astype(BF16)
            shifted[3, at : at + ROW, :] = pltpu.roll(block, ROW - 2, 0).astype(BF16)
            tiles_x.append(block)
            tiles_g.append(jnp.concatenate([gbuf[:, j * PAIR : (j + 1) * PAIR].astype(F32), pad], axis=0))
        lanes = slice(pair * PAIR, (pair + 1) * PAIR)
        lhs_t[0:PAIR, lanes] = jnp.concatenate(tiles_x, axis=0).T.astype(BF16)
        lhs_t[PAIR : 2 * PAIR, lanes] = jnp.concatenate(tiles_g, axis=0).T.astype(BF16)

    def product(d, s, part):
        left = lhs_t[...] if part is None else lhs_t[part * PAIR : (part + 1) * PAIR, :]
        right = [shifted[d, (1 + one) * ROW : (1 + one) * ROW + rows, :] for one in s]
        right = right[0] if len(right) == 1 else jnp.concatenate(right, axis=1)
        full = jnp.dot(left, right, preferred_element_type=F32)
        return [full[:, k * PAIR : (k + 1) * PAIR] for k in range(len(s))]

    def table(at_s, base, s):
        upper = at_s[s][base : base + C, :]
        here = pltpu.roll(at_s[s][base + C : base + PAIR, :], C, 1)
        if s + 1 not in at_s:
            return upper + here
        after = pltpu.roll(at_s[s + 1][base + C : base + PAIR, :], C, 1)
        return upper + jnp.where(low, here, after)

    def odd(at_s, base, s):
        return at_s[s][base : base + C, :] + pltpu.roll(at_s[s + 1][base + C : base + PAIR, :], C, 1)

    def store(name, value):
        index = PLACE[name]
        slot = slot_of(index // QUART, layer, first, second)
        at = index % QUART * ROW
        out_ref[slot, at : at + ROW, :] = value

    row = lax.broadcasted_iota(jnp.int32, (ROW, PAIR), 0)
    col = lax.rem(lax.broadcasted_iota(jnp.int32, (ROW, PAIR), 1), C)
    pack = lambda a, b: jnp.where(row >= col, a, b)
    diagonal = lambda a: jnp.sum(jnp.where(row == col, a, 0.0), axis=0, keepdims=True)

    p = product(0, (-1, 0), 1) + product(0, (1,), 1)
    at_s = dict(zip((-1, 0, 1), p))
    store("w0z", table(at_s, 0, 0))
    w0 = odd(at_s, 0, -1)
    p = product(1, (-1, 0), None) + product(1, (1,), None)
    at_s = dict(zip((-1, 0, 1), p))
    x0z = table(at_s, 0, 0)
    store("h0", jnp.where(low, table(at_s, 0, 1), w0))
    store("w1z", table(at_s, PAIR, 0))
    w1 = odd(at_s, PAIR, -1)
    p = product(2, (-1, 0), None) + product(2, (1,), None)
    at_s = dict(zip((-1, 0, 1), p))
    store("x1m", table(at_s, 0, -1))
    store("x1z", table(at_s, 0, 0))
    x12 = table(at_s, 0, 1)
    store("w2z", table(at_s, PAIR, 0))
    w2 = odd(at_s, PAIR, -1)
    p = product(3, (-1, 0), 0) + product(3, (1,), 0)
    at_s = dict(zip((-1, 0, 1), p))
    store("x2m", table(at_s, 0, -1))
    store("x2z", table(at_s, 0, 0))
    store("x22", jnp.where(low, x12, pltpu.roll(table(at_s, 0, 1), C, 1)))
    gl = lhs_t[PAIR : 2 * PAIR, :]
    gg = lax.dot_general(gl, gl, (((1,), (1,)), ((), ())), preferred_element_type=F32)
    gx = jnp.where(low, gg[0:C, :] + pltpu.roll(gg[C:PAIR, :], C, 1), pltpu.roll(x0z, C, 1))
    fl = [
        jnp.where(
            low,
            shifted[d, ROW : 2 * ROW, :].astype(F32),
            shifted[d, rows : ROW + rows, :].astype(F32),
        ).astype(BF16)
        for d in (1, 2, 3)
    ]
    for d, name in enumerate(("cg", "cc1", "cc2")):
        q = contract0(fl[0], fl[d])
        both = jnp.where(low, q[0:C, :], q[C:PAIR, :])
        if d == 0:
            name, both = "cg", pack(both, gx)
        store(name, both)
    line = lax.broadcasted_iota(jnp.int32, (n_edge, PAIR), 0)
    lane = lax.broadcasted_iota(jnp.int32, (n_edge, PAIR), 1)
    corner = ((line == 0) & (lane < C)) | ((line == wp - 1) & (lane >= C))
    halves = []
    lines = []
    corners = []
    for e in range(2):
        zero = edges[e, 8 : 8 + n_edge, :]
        here = zero.astype(BF16)
        after = edges[e, 9 : 9 + n_edge, :].astype(BF16)
        at_s = {0: contract0(here, here), 1: contract0(here, after)}
        lines.append(table(at_s, 0, 0))
        halves.append(table(at_s, 0, 1))
        only = jnp.where(corner, zero, 0.0).astype(BF16)
        q = contract0(only, only)
        corners.append(jnp.where(low, q[0:C, :], q[C:PAIR, :]))
    store("h1", jnp.where(low, halves[0], w1))
    store("h2", jnp.where(low, halves[1], w2))
    store("kk", pack(corners[0], corners[1]))
    store("r01", jnp.where(low, pltpu.roll(lines[0], C, 1), lines[1]))
    rx = jnp.where(low, pack(lines[0], lines[1]), x0z)
    diags = jnp.concatenate(
        [diagonal(corners[1]), diagonal(gx), diagonal(lines[1]), jnp.zeros((5, PAIR), F32)], axis=0
    )
    for quarter in range(4):
        slot = slot_of(quarter, layer, first, second)
        out_ref[slot, LAST:DIAGS, :] = rx[quarter * PIECE : (quarter + 1) * PIECE, :]
        out_ref[slot, DIAGS:QROWS, :] = diags
    if not own:
        copies[2].wait()
        copies[3].wait()


def local_sums(height, width, own, x, g):
    wp = width // 2
    sums = jax.ShapeDtypeStruct((4, QROWS, PAIR), F32)
    image = jax.ShapeDtypeStruct((height, width * C), BF16)
    n_edge = (wp + 15) // 16 * 16
    vmem = pl.BlockSpec(memory_space=pltpu.VMEM)
    scratch = [
        pltpu.VMEM((4, (wp + 2) * ROW, PAIR), BF16),
        pltpu.VMEM((2 * PAIR, wp * ROW), BF16),
        pltpu.VMEM((2, n_edge + 16, PAIR), F32),
    ]
    if not own:
        scratch = [pltpu.VMEM(image.shape, BF16)] * 2 + scratch + [pltpu.SemaphoreType.DMA((4,))]
    return pl.pallas_call(
        functools.partial(local_kernel, height, width, own),
        out_shape=sums if own else (sums, image, image),
        in_specs=[vmem if own else pl.BlockSpec(memory_space=pltpu.HBM)] * 2,
        out_specs=vmem if own else (vmem,) * 3,
        scratch_shapes=scratch,
        compiler_params=pltpu.CompilerParams(vmem_limit_bytes=SUMS_VMEM),
    )(x, g)


def split(a):
    high = a.astype(BF16)
    return high, (a - high.astype(F32)).astype(BF16)


def dot3(a, b):
    ah, al = split(a)
    bh, bl = split(b)
    dot = functools.partial(jnp.dot, preferred_element_type=F32)
    return dot(ah, bh) + (dot(ah, bl) + dot(al, bh))


def normalized(m):
    n = m.shape[0]
    diag = lax.broadcasted_iota(jnp.int32, (n, n), 0) == lax.broadcasted_iota(jnp.int32, (n, n), 1)
    trace = jnp.sum(jnp.where(diag, m, 0.0))
    m = m + jnp.where(diag, DAMP * trace / n, 0.0)
    inv = lax.rsqrt(jnp.sum(m * m))
    return jnp.where(diag, 1.0, 0.0) - m * inv, inv


def final_kernel(total_rows, own_ref, beside_ref, below_ref, across_ref, out_ref, quarters, m_hi, m_lo):
    _, first, second = chip_place()
    for slot, ref in enumerate((own_ref, beside_ref, below_ref, across_ref)):
        quarters[slot] = ref[...]

    def slot(quarter):
        return gathered_slot(quarter, first, second)

    def load(name):
        index = PLACE[name]
        at = index % QUART * ROW
        both = quarters[slot(index // QUART), at : at + ROW, :]
        return both[:, 0:C], both[:, C:PAIR]

    row = lax.broadcasted_iota(jnp.int32, (C, C), 0)
    col = lax.broadcasted_iota(jnp.int32, (C, C), 1)
    diags = quarters[slot(0), DIAGS:QROWS, :]

    def unpack(block, line, at):
        flipped = block.T
        mirrored = jnp.where(row < col, block, flipped)
        diagonal = jnp.broadcast_to(diags[line : line + 1, at : at + C], (C, C))
        return jnp.where(row >= col, block, flipped), jnp.where(row == col, diagonal, mirrored)

    rx = jnp.concatenate([quarters[slot(quarter), LAST:DIAGS, :] for quarter in range(4)], axis=0)
    x0 = {1: rx[:, C:PAIR]}
    row0 = {}
    row1 = {}
    col0 = {}
    col1 = {}
    row0[0], row1[0] = unpack(rx[:, 0:C], 2, 0)
    row0[1], row1[1] = load("r01")
    x0[2], w00 = load("h0")
    row0[2], w10 = load("h1")
    row1[2], w20 = load("h2")
    low, high = load("cg")
    col0[0], g = unpack(low, 1, 0)
    col1[0], x0[0] = unpack(high, 1, C)
    low, high = load("kk")
    k00, k10 = unpack(low, 0, 0)
    k01, k11 = unpack(high, 0, C)
    corner = (k00, k01, k10, k11)
    down = {}
    for dr in (1, 2):
        down[dr, -2], down[dr, -1] = load("x%dm" % dr)
        down[dr, 0], down[dr, 1] = load("x%dz" % dr)
        col0[dr], col1[dr] = load("cc%d" % dr)
    down[1, 2], down[2, 2] = load("x22")

    squares = []

    def put(t, u, block):
        high, rest = split(block)
        m_hi[t * C : (t + 1) * C, u * C : (u + 1) * C] = high
        m_lo[t * C : (t + 1) * C, u * C : (u + 1) * C] = rest

    def put_all(taps, block):
        squares.append(2.0 * len(taps) * (block * block))
        for t, u in taps:
            put(t, u, block)
        flipped = block.T
        for t, u in taps:
            put(u, t, flipped)

    on_diagonal = []
    for a in range(3):
        line = {}
        for dc in range(3):
            line[dc] = x0[dc] - row1[dc] if a == 0 else (x0[dc] - row0[dc] if a == 2 else x0[dc])
        for b in range(3):
            block = line[0]
            if b == 0:
                block = block - col1[0]
                if a == 0:
                    block = block + corner[3]
                if a == 2:
                    block = block + corner[1]
            if b == 2:
                block = block - col0[0]
                if a == 0:
                    block = block + corner[2]
                if a == 2:
                    block = block + corner[0]
            squares.append(block * block)
            on_diagonal.append(block)
            put(3 * a + b, 3 * a + b, block)
        put_all([(3 * a, 3 * a + 1), (3 * a + 1, 3 * a + 2)], line[1])
        put_all([(3 * a, 3 * a + 2)], line[2])
    for dr in (1, 2):
        starts = range(3 - dr)
        for b in range(3):
            block = down[dr, 0]
            if b == 0:
                block = block - col1[dr]
            if b == 2:
                block = block - col0[dr]
            put_all([(3 * a + b, 3 * (a + dr) + b) for a in starts], block)
        for dc in (-2, -1, 1, 2):
            taps = [(3 * a + b, 3 * (a + dr) + b + dc) for a in starts for b in range(3) if 0 <= b + dc < 3]
            put_all(taps, down[dr, dc])

    n = TAPS * C
    trace = jnp.sum(jnp.where(row == col, sum(on_diagonal), 0.0))
    shift = DAMP * trace / n
    inv_a = lax.rsqrt(jnp.sum(sum(squares)) + shift * (2.0 * trace + n * shift))
    keep = 1.0 - inv_a * shift
    eg, inv_g = normalized(g)
    eg2 = dot3(eg, eg)
    pg = eg + dot3(eg, eg2) + eg2
    w0 = load("w0z")
    w1 = load("w1z")
    w2 = load("w2z")
    w = jnp.concatenate([w00, w0[0], w0[1], w10, w1[0], w1[1], w20, w2[0], w2[1]], axis=1)
    w = w + dot3(pg, w)
    v = w.T * (inv_a * inv_g * total_rows)

    def apply(v):
        vh, vl = split(v)
        both = jnp.dot(m_hi[...], jnp.concatenate([vh, vl], axis=1), preferred_element_type=F32)
        mv = both[:, 0:C] + (both[:, C:PAIR] + jnp.dot(m_lo[...], vh, preferred_element_type=F32))
        return keep * v - inv_a * mv

    v = v + apply(v)
    v = v + apply(apply(v))
    out_ref[...] = v.T


def precondition(parts, total_rows):
    n = TAPS * C
    return pl.pallas_call(
        functools.partial(final_kernel, float(total_rows)),
        out_shape=jax.ShapeDtypeStruct((C, n), F32),
        in_specs=[pl.BlockSpec(memory_space=pltpu.VMEM)] * 4,
        out_specs=pl.BlockSpec(memory_space=pltpu.VMEM),
        scratch_shapes=[
            pltpu.VMEM((4, QROWS, PAIR), F32),
            pltpu.VMEM((n, n), BF16),
            pltpu.VMEM((n, n), BF16),
        ],
        compiler_params=pltpu.CompilerParams(vmem_limit_bytes=VMEM_LIMIT),
    )(*parts)


def pairings(n_dp, n_grp):
    n = n_dp * n_grp
    core_bit = n_grp
    first, second = 1, 2 * n_grp
    doublings = []
    bit = 4 * n_grp
    while bit < n:
        doublings.append(bit)
        bit *= 2
    orders = ([first, second] + doublings, [second, first] + doublings[::-1])
    pairs = lambda masks: [(i, i ^ masks[1 if i & core_bit else 0]) for i in range(n)]
    rounds = [pairs(masks) for masks in zip(*orders)]
    return pairs((core_bit, core_bit)), rounds[:2], rounds[2:], (pairs((first, first)), pairs((second, second)), pairs((first + second, first + second)))


def shards(feature_maps, output_grads):
    n_dp, n_grp = lax.axis_size("dp"), lax.axis_size("grp")
    cores, halvings, doublings, gathers = pairings(n_dp, n_grp)
    swap = lambda a, p: lax.ppermute(a, ("dp", "grp"), p)
    total_rows = feature_maps.shape[2] * feature_maps.shape[3] // C * feature_maps.shape[1] * n_dp * n_grp
    height = feature_maps.shape[2]
    width = feature_maps.shape[3] // C
    send, own_x, own_g = local_sums(height, width, False, feature_maps, output_grads)
    got = swap(send, cores)
    keep = local_sums(height, width, True, own_x, own_g)
    far_next = swap(keep[3] + got[3], halvings[0])
    far_own = swap(keep[2] + got[2], halvings[0])
    got_next = swap(keep[1] + got[1] + far_next, halvings[1])
    own = keep[0] + got[0] + far_own + got_next
    for p in doublings:
        own = own + swap(own, p)
    beside = swap(own, gathers[0])
    below = swap(own, gathers[1])
    across = swap(own, gathers[2])
    mine = precondition((own, beside, below, across), total_rows)
    other = swap(mine, cores)
    core = lax.rem(lax.axis_index("dp"), 2)
    return jnp.where(core == 0, jnp.stack([mine, other]), jnp.stack([other, mine]))


def solution(mesh):
    placed = (P(None, ("dp", "grp"), None, None), P(None, ("dp", "grp"), None, None))
    return jax.shard_map(shards, mesh=mesh, in_specs=placed, out_specs=P(), check_vma=False)
```

```python
import functools

import jax
import jax.numpy as jnp
import numpy as np
from jax import lax
from jax.experimental import pallas as pl
from jax.experimental.pallas import tpu as pltpu
from jax.sharding import PartitionSpec as P

C = 64
TAPS = 9
PAIR = 2 * C
ROW = 64
QUART = 4
DAMP = 0.1
SUMS_VMEM = 52 * 2**20
VMEM_LIMIT = 48 * 2**20
F32 = jnp.float32
BF16 = jnp.bfloat16

PAIRS = (
    "x1m", "x1z", "cc1", "x2m",
    "x2z", "cc2", "x22", "kk",
    "cg", "w0z", "w1z", "w2z",
    "h0", "h1", "h2", "r01",
)
PLACE = {name: index for index, name in enumerate(PAIRS)}
LAST = QUART * ROW
PIECE = ROW // 4
DIAGS = LAST + PIECE
QROWS = DIAGS + 8


def contract0(a, b):
    return lax.dot_general(a, b, (((0,), (0,)), ((), ())), preferred_element_type=F32)


def chip_place():
    dp = lax.axis_index("dp")
    core = lax.rem(dp, 2)
    second = lax.rem(dp // 2, 2)
    first = lax.axis_index("grp")
    return core, first, second


def slot_of(quarter, layer, first, second):
    mine_first = first ^ (quarter // 2)
    mine_second = second ^ (quarter % 2)
    major = jnp.where(layer == 0, mine_first, mine_second)
    minor = jnp.where(layer == 0, mine_second, mine_first)
    return 2 * major + minor


def gathered_slot(quarter, first, second):
    return 2 * (second ^ (quarter % 2)) + (first ^ (quarter // 2))


def local_kernel(height, width, own, *refs):
    if own:
        xbuf, gbuf, out_ref, shifted, lhs_t, edges = refs
    else:
        x_hbm, g_hbm, out_ref, next_x, next_g, xbuf, gbuf, shifted, lhs_t, edges, sems = refs
    core, first, second = chip_place()
    wp = width // 2
    rows = wp * ROW
    layer = core if own else 1 - core
    if not own:
        copies = [
            pltpu.make_async_copy(x_hbm.at[layer, 0], xbuf, sems.at[0]),
            pltpu.make_async_copy(g_hbm.at[layer, 0], gbuf, sems.at[1]),
            pltpu.make_async_copy(x_hbm.at[core, 0], next_x, sems.at[2]),
            pltpu.make_async_copy(g_hbm.at[core, 0], next_g, sems.at[3]),
        ]
        for one in copies:
            one.start()
    for d in range(4):
        shifted[d, 0:ROW, :] = jnp.zeros((ROW, PAIR), BF16)
        shifted[d, ROW + rows : 2 * ROW + rows, :] = jnp.zeros((ROW, PAIR), BF16)
    edges[...] = jnp.zeros_like(edges)
    low = lax.broadcasted_iota(jnp.int32, (ROW, PAIR), 1) < C
    pad = jnp.zeros((ROW - height, PAIR), F32)
    n_edge = edges.shape[1] - 16
    if not own:
        copies[0].wait()
        copies[1].wait()
    for pair in range(wp // 2):
        tiles_x = []
        tiles_g = []
        for half in range(2):
            j = 2 * pair + half
            block = jnp.concatenate([xbuf[:, j * PAIR : (j + 1) * PAIR].astype(F32), pad], axis=0)
            at = ROW + j * ROW
            edges[0, 8 + j : 9 + j, :] = block[0:1, :]
            edges[1, 8 + j : 9 + j, :] = block[height - 1 : height, :]
            shifted[0, at : at + ROW, :] = pltpu.roll(block, 1, 0).astype(BF16)
            shifted[1, at : at + ROW, :] = block.astype(BF16)
            shifted[2, at : at + ROW, :] = pltpu.roll(block, ROW - 1, 0).astype(BF16)
            shifted[3, at : at + ROW, :] = pltpu.roll(block, ROW - 2, 0).astype(BF16)
            tiles_x.append(block)
            tiles_g.append(jnp.concatenate([gbuf[:, j * PAIR : (j + 1) * PAIR].astype(F32), pad], axis=0))
        lanes = slice(pair * PAIR, (pair + 1) * PAIR)
        lhs_t[0:PAIR, lanes] = jnp.concatenate(tiles_x, axis=0).T.astype(BF16)
        lhs_t[PAIR : 2 * PAIR, lanes] = jnp.concatenate(tiles_g, axis=0).T.astype(BF16)

    def product(wanted, part):
        left = lhs_t[...] if part is None else lhs_t[part * PAIR : (part + 1) * PAIR, :]
        right = [shifted[d, (1 + s) * ROW : (1 + s) * ROW + rows, :] for d, s in wanted]
        full = jnp.dot(left, right[0] if len(right) == 1 else jnp.concatenate(right, axis=1), preferred_element_type=F32)
        return [full[:, k * PAIR : (k + 1) * PAIR] for k in range(len(right))]

    def table(at_s, base, s):
        upper = at_s[s][base : base + C, :]
        here = pltpu.roll(at_s[s][base + C : base + PAIR, :], C, 1)
        if s + 1 not in at_s:
            return upper + here
        after = pltpu.roll(at_s[s + 1][base + C : base + PAIR, :], C, 1)
        return upper + jnp.where(low, here, after)

    def odd(at_s, base, s):
        return at_s[s][base : base + C, :] + pltpu.roll(at_s[s + 1][base + C : base + PAIR, :], C, 1)

    def store(name, value):
        index = PLACE[name]
        slot = slot_of(index // QUART, layer, first, second)
        at = index % QUART * ROW
        out_ref[slot, at : at + ROW, :] = value

    row = lax.broadcasted_iota(jnp.int32, (ROW, PAIR), 0)
    col = lax.rem(lax.broadcasted_iota(jnp.int32, (ROW, PAIR), 1), C)
    pack = lambda a, b: jnp.where(row >= col, a, b)
    diagonal = lambda a: jnp.sum(jnp.where(row == col, a, 0.0), axis=0, keepdims=True)

    p = product(((0, -1), (0, 0)), 1) + product(((0, 1),), 1)
    at_s = dict(zip((-1, 0, 1), p))
    store("w0z", table(at_s, 0, 0))
    w0 = odd(at_s, 0, -1)
    same, under = product(((1, 1), (2, 1)), None)
    p = product(((1, -1), (1, 0)), None)
    at_s = dict(zip((-1, 0, 1), p + [same]))
    x0z = table(at_s, 0, 0)
    store("h0", jnp.where(low, table(at_s, 0, 1), w0))
    store("w1z", table(at_s, PAIR, 0))
    w1 = odd(at_s, PAIR, -1)
    p = product(((2, -1), (2, 0)), None)
    at_s = dict(zip((-1, 0, 1), p + [under]))
    store("x1m", table(at_s, 0, -1))
    store("x1z", table(at_s, 0, 0))
    x12 = table(at_s, 0, 1)
    store("w2z", table(at_s, PAIR, 0))
    w2 = odd(at_s, PAIR, -1)
    p = product(((3, -1), (3, 0)), 0) + product(((3, 1),), 0)
    at_s = dict(zip((-1, 0, 1), p))
    store("x2m", table(at_s, 0, -1))
    store("x2z", table(at_s, 0, 0))
    store("x22", jnp.where(low, x12, pltpu.roll(table(at_s, 0, 1), C, 1)))
    gl = lhs_t[PAIR : 2 * PAIR, :]
    gg = lax.dot_general(gl, gl, (((1,), (1,)), ((), ())), preferred_element_type=F32)
    gx = jnp.where(low, gg[0:C, :] + pltpu.roll(gg[C:PAIR, :], C, 1), pltpu.roll(x0z, C, 1))
    fl = [
        jnp.where(
            low,
            shifted[d, ROW : 2 * ROW, :].astype(F32),
            shifted[d, rows : ROW + rows, :].astype(F32),
        ).astype(BF16)
        for d in (1, 2, 3)
    ]
    for d, name in enumerate(("cg", "cc1", "cc2")):
        q = contract0(fl[0], fl[d])
        both = jnp.where(low, q[0:C, :], q[C:PAIR, :])
        if d == 0:
            name, both = "cg", pack(both, gx)
        store(name, both)
    line = lax.broadcasted_iota(jnp.int32, (n_edge, PAIR), 0)
    lane = lax.broadcasted_iota(jnp.int32, (n_edge, PAIR), 1)
    corner = ((line == 0) & (lane < C)) | ((line == wp - 1) & (lane >= C))
    halves = []
    lines = []
    corners = []
    for e in range(2):
        zero = edges[e, 8 : 8 + n_edge, :]
        here = zero.astype(BF16)
        after = edges[e, 9 : 9 + n_edge, :].astype(BF16)
        at_s = {0: contract0(here, here), 1: contract0(here, after)}
        lines.append(table(at_s, 0, 0))
        halves.append(table(at_s, 0, 1))
        only = jnp.where(corner, zero, 0.0).astype(BF16)
        q = contract0(only, only)
        corners.append(jnp.where(low, q[0:C, :], q[C:PAIR, :]))
    store("h1", jnp.where(low, halves[0], w1))
    store("h2", jnp.where(low, halves[1], w2))
    store("kk", pack(corners[0], corners[1]))
    store("r01", jnp.where(low, pltpu.roll(lines[0], C, 1), lines[1]))
    rx = jnp.where(low, pack(lines[0], lines[1]), x0z)
    diags = jnp.concatenate(
        [diagonal(corners[1]), diagonal(gx), diagonal(lines[1]), jnp.zeros((5, PAIR), F32)], axis=0
    )
    for quarter in range(4):
        slot = slot_of(quarter, layer, first, second)
        out_ref[slot, LAST:DIAGS, :] = rx[quarter * PIECE : (quarter + 1) * PIECE, :]
        out_ref[slot, DIAGS:QROWS, :] = diags
    if not own:
        copies[2].wait()
        copies[3].wait()


def local_sums(height, width, own, x, g):
    wp = width // 2
    sums = jax.ShapeDtypeStruct((4, QROWS, PAIR), F32)
    image = jax.ShapeDtypeStruct((height, width * C), BF16)
    n_edge = (wp + 15) // 16 * 16
    vmem = pl.BlockSpec(memory_space=pltpu.VMEM)
    scratch = [
        pltpu.VMEM((4, (wp + 2) * ROW, PAIR), BF16),
        pltpu.VMEM((2 * PAIR, wp * ROW), BF16),
        pltpu.VMEM((2, n_edge + 16, PAIR), F32),
    ]
    if not own:
        scratch = [pltpu.VMEM(image.shape, BF16)] * 2 + scratch + [pltpu.SemaphoreType.DMA((4,))]
    return pl.pallas_call(
        functools.partial(local_kernel, height, width, own),
        out_shape=sums if own else (sums, image, image),
        in_specs=[vmem if own else pl.BlockSpec(memory_space=pltpu.HBM)] * 2,
        out_specs=vmem if own else (vmem,) * 3,
        scratch_shapes=scratch,
        compiler_params=pltpu.CompilerParams(vmem_limit_bytes=SUMS_VMEM),
    )(x, g)


def split(a):
    high = a.astype(BF16)
    return high, (a - high.astype(F32)).astype(BF16)


def dot3(a, b):
    ah, al = split(a)
    bh, bl = split(b)
    dot = functools.partial(jnp.dot, preferred_element_type=F32)
    return dot(ah, bh) + (dot(ah, bl) + dot(al, bh))


def normalized(m):
    n = m.shape[0]
    diag = lax.broadcasted_iota(jnp.int32, (n, n), 0) == lax.broadcasted_iota(jnp.int32, (n, n), 1)
    trace = jnp.sum(jnp.where(diag, m, 0.0))
    m = m + jnp.where(diag, DAMP * trace / n, 0.0)
    inv = lax.rsqrt(jnp.sum(m * m))
    return jnp.where(diag, 1.0, 0.0) - m * inv, inv


def final_kernel(total_rows, own_ref, beside_ref, below_ref, across_ref, out_ref, quarters, m_hi, m_lo):
    _, first, second = chip_place()
    for slot, ref in enumerate((own_ref, beside_ref, below_ref, across_ref)):
        quarters[slot] = ref[...]

    def slot(quarter):
        return gathered_slot(quarter, first, second)

    def load(name):
        index = PLACE[name]
        at = index % QUART * ROW
        both = quarters[slot(index // QUART), at : at + ROW, :]
        return both[:, 0:C], both[:, C:PAIR]

    row = lax.broadcasted_iota(jnp.int32, (C, C), 0)
    col = lax.broadcasted_iota(jnp.int32, (C, C), 1)
    diags = quarters[slot(0), DIAGS:QROWS, :]

    def unpack(block, line, at):
        flipped = block.T
        mirrored = jnp.where(row < col, block, flipped)
        diagonal = jnp.broadcast_to(diags[line : line + 1, at : at + C], (C, C))
        return jnp.where(row >= col, block, flipped), jnp.where(row == col, diagonal, mirrored)

    rx = jnp.concatenate([quarters[slot(quarter), LAST:DIAGS, :] for quarter in range(4)], axis=0)
    x0 = {1: rx[:, C:PAIR]}
    row0 = {}
    row1 = {}
    col0 = {}
    col1 = {}
    row0[0], row1[0] = unpack(rx[:, 0:C], 2, 0)
    row0[1], row1[1] = load("r01")
    x0[2], w00 = load("h0")
    row0[2], w10 = load("h1")
    row1[2], w20 = load("h2")
    low, high = load("cg")
    col0[0], g = unpack(low, 1, 0)
    col1[0], x0[0] = unpack(high, 1, C)
    low, high = load("kk")
    k00, k10 = unpack(low, 0, 0)
    k01, k11 = unpack(high, 0, C)
    corner = (k00, k01, k10, k11)
    down = {}
    for dr in (1, 2):
        down[dr, -2], down[dr, -1] = load("x%dm" % dr)
        down[dr, 0], down[dr, 1] = load("x%dz" % dr)
        col0[dr], col1[dr] = load("cc%d" % dr)
    down[1, 2], down[2, 2] = load("x22")

    squares = []

    def put(t, u, block):
        high, rest = split(block)
        m_hi[t * C : (t + 1) * C, u * C : (u + 1) * C] = high
        m_lo[t * C : (t + 1) * C, u * C : (u + 1) * C] = rest

    def put_all(taps, block):
        squares.append(2.0 * len(taps) * (block * block))
        for t, u in taps:
            put(t, u, block)
        flipped = block.T
        for t, u in taps:
            put(u, t, flipped)

    on_diagonal = []
    for a in range(3):
        line = {}
        for dc in range(3):
            line[dc] = x0[dc] - row1[dc] if a == 0 else (x0[dc] - row0[dc] if a == 2 else x0[dc])
        for b in range(3):
            block = line[0]
            if b == 0:
                block = block - col1[0]
                if a == 0:
                    block = block + corner[3]
                if a == 2:
                    block = block + corner[1]
            if b == 2:
                block = block - col0[0]
                if a == 0:
                    block = block + corner[2]
                if a == 2:
                    block = block + corner[0]
            squares.append(block * block)
            on_diagonal.append(block)
            put(3 * a + b, 3 * a + b, block)
        put_all([(3 * a, 3 * a + 1), (3 * a + 1, 3 * a + 2)], line[1])
        put_all([(3 * a, 3 * a + 2)], line[2])
    for dr in (1, 2):
        starts = range(3 - dr)
        for b in range(3):
            block = down[dr, 0]
            if b == 0:
                block = block - col1[dr]
            if b == 2:
                block = block - col0[dr]
            put_all([(3 * a + b, 3 * (a + dr) + b) for a in starts], block)
        for dc in (-2, -1, 1, 2):
            taps = [(3 * a + b, 3 * (a + dr) + b + dc) for a in starts for b in range(3) if 0 <= b + dc < 3]
            put_all(taps, down[dr, dc])

    n = TAPS * C
    trace = jnp.sum(jnp.where(row == col, sum(on_diagonal), 0.0))
    shift = DAMP * trace / n
    inv_a = lax.rsqrt(jnp.sum(sum(squares)) + shift * (2.0 * trace + n * shift))
    keep = 1.0 - inv_a * shift
    eg, inv_g = normalized(g)
    eg2 = dot3(eg, eg)
    pg = eg + dot3(eg, eg2) + eg2
    w0 = load("w0z")
    w1 = load("w1z")
    w2 = load("w2z")
    w = jnp.concatenate([w00, w0[0], w0[1], w10, w1[0], w1[1], w20, w2[0], w2[1]], axis=1)
    w = w + dot3(pg, w)
    v = w.T * (inv_a * inv_g * total_rows)

    def apply(v):
        vh, vl = split(v)
        both = jnp.dot(m_hi[...], jnp.concatenate([vh, vl], axis=1), preferred_element_type=F32)
        mv = both[:, 0:C] + (both[:, C:PAIR] + jnp.dot(m_lo[...], vh, preferred_element_type=F32))
        return keep * v - inv_a * mv

    v = v + apply(v)
    v = v + apply(apply(v))
    out_ref[...] = v.T


def precondition(parts, total_rows):
    n = TAPS * C
    return pl.pallas_call(
        functools.partial(final_kernel, float(total_rows)),
        out_shape=jax.ShapeDtypeStruct((C, n), F32),
        in_specs=[pl.BlockSpec(memory_space=pltpu.VMEM)] * 4,
        out_specs=pl.BlockSpec(memory_space=pltpu.VMEM),
        scratch_shapes=[
            pltpu.VMEM((4, QROWS, PAIR), F32),
            pltpu.VMEM((n, n), BF16),
            pltpu.VMEM((n, n), BF16),
        ],
        compiler_params=pltpu.CompilerParams(vmem_limit_bytes=VMEM_LIMIT),
    )(*parts)


def pairings(n_dp, n_grp):
    n = n_dp * n_grp
    core_bit = n_grp
    first, second = 1, 2 * n_grp
    doublings = []
    bit = 4 * n_grp
    while bit < n:
        doublings.append(bit)
        bit *= 2
    orders = ([first, second] + doublings, [second, first] + doublings[::-1])
    pairs = lambda masks: [(i, i ^ masks[1 if i & core_bit else 0]) for i in range(n)]
    rounds = [pairs(masks) for masks in zip(*orders)]
    return pairs((core_bit, core_bit)), rounds[:2], rounds[2:], (pairs((first, first)), pairs((second, second)), pairs((first + second, first + second)))


def shards(feature_maps, output_grads):
    n_dp, n_grp = lax.axis_size("dp"), lax.axis_size("grp")
    cores, halvings, doublings, gathers = pairings(n_dp, n_grp)
    swap = lambda a, p: lax.ppermute(a, ("dp", "grp"), p)
    total_rows = feature_maps.shape[2] * feature_maps.shape[3] // C * feature_maps.shape[1] * n_dp * n_grp
    height = feature_maps.shape[2]
    width = feature_maps.shape[3] // C
    send, own_x, own_g = local_sums(height, width, False, feature_maps, output_grads)
    got = swap(send, cores)
    keep = local_sums(height, width, True, own_x, own_g)
    far_next = swap(keep[3] + got[3], halvings[0])
    far_own = swap(keep[2] + got[2], halvings[0])
    got_next = swap(keep[1] + got[1] + far_next, halvings[1])
    own = keep[0] + got[0] + far_own + got_next
    for p in doublings:
        own = own + swap(own, p)
    beside = swap(own, gathers[0])
    below = swap(own, gathers[1])
    across = swap(own, gathers[2])
    mine = precondition((own, beside, below, across), total_rows)
    other = swap(mine, cores)
    core = lax.rem(lax.axis_index("dp"), 2)
    return jnp.where(core == 0, jnp.stack([mine, other]), jnp.stack([other, mine]))


def solution(mesh):
    placed = (P(None, ("dp", "grp"), None, None), P(None, ("dp", "grp"), None, None))
    return jax.shard_map(shards, mesh=mesh, in_specs=placed, out_specs=P(), check_vma=False)
```

```python
import functools

import jax
import jax.numpy as jnp
import numpy as np
from jax import lax
from jax.experimental import pallas as pl
from jax.experimental.pallas import tpu as pltpu
from jax.sharding import PartitionSpec as P

C = 64
TAPS = 9
PAIR = 2 * C
ROW = 64
QUART = 4
DAMP = 0.1
SUMS_VMEM = 52 * 2**20
VMEM_LIMIT = 48 * 2**20
F32 = jnp.float32
BF16 = jnp.bfloat16

PAIRS = (
    "x1m", "x1z", "cc1", "x2m",
    "x2z", "cc2", "x22", "kk",
    "cg", "w0z", "w1z", "w2z",
    "h0", "h1", "h2", "r01",
)
PLACE = {name: index for index, name in enumerate(PAIRS)}
LAST = QUART * ROW
PIECE = ROW // 4
DIAGS = LAST + PIECE
QROWS = DIAGS + 8


def contract0(a, b):
    return lax.dot_general(a, b, (((0,), (0,)), ((), ())), preferred_element_type=F32)


def chip_place():
    dp = lax.axis_index("dp")
    core = lax.rem(dp, 2)
    second = lax.rem(dp // 2, 2)
    first = lax.axis_index("grp")
    return core, first, second


def slot_of(quarter, layer, first, second):
    mine_first = first ^ (quarter // 2)
    mine_second = second ^ (quarter % 2)
    major = jnp.where(layer == 0, mine_first, mine_second)
    minor = jnp.where(layer == 0, mine_second, mine_first)
    return 2 * major + minor


def gathered_slot(quarter, first, second):
    return 2 * (second ^ (quarter % 2)) + (first ^ (quarter // 2))


def local_kernel(height, width, own, *refs):
    if own:
        xbuf, gbuf, out_ref, shifted, lhs_t, edges = refs
    else:
        x_hbm, g_hbm, out_ref, next_x, next_g, xbuf, gbuf, shifted, lhs_t, edges, sems = refs
    core, first, second = chip_place()
    wp = width // 2
    rows = wp * ROW
    layer = core if own else 1 - core
    if not own:
        copies = [
            pltpu.make_async_copy(x_hbm.at[layer, 0], xbuf, sems.at[0]),
            pltpu.make_async_copy(g_hbm.at[layer, 0], gbuf, sems.at[1]),
            pltpu.make_async_copy(x_hbm.at[core, 0], next_x, sems.at[2]),
            pltpu.make_async_copy(g_hbm.at[core, 0], next_g, sems.at[3]),
        ]
        for one in copies:
            one.start()
    for d in range(4):
        shifted[d, 0:ROW, :] = jnp.zeros((ROW, PAIR), BF16)
        shifted[d, ROW + rows : 2 * ROW + rows, :] = jnp.zeros((ROW, PAIR), BF16)
    edges[...] = jnp.zeros_like(edges)
    low = lax.broadcasted_iota(jnp.int32, (ROW, PAIR), 1) < C
    pad = jnp.zeros((ROW - height, PAIR), F32)
    n_edge = edges.shape[1] - 16
    if not own:
        copies[0].wait()
        copies[1].wait()
    for pair in range(wp // 2):
        tiles_x = []
        tiles_g = []
        for half in range(2):
            j = 2 * pair + half
            block = jnp.concatenate([xbuf[:, j * PAIR : (j + 1) * PAIR].astype(F32), pad], axis=0)
            at = ROW + j * ROW
            edges[0, 8 + j : 9 + j, :] = block[0:1, :]
            edges[1, 8 + j : 9 + j, :] = block[height - 1 : height, :]
            shifted[0, at : at + ROW, :] = pltpu.roll(block, 1, 0).astype(BF16)
            shifted[1, at : at + ROW, :] = block.astype(BF16)
            shifted[2, at : at + ROW, :] = pltpu.roll(block, ROW - 1, 0).astype(BF16)
            shifted[3, at : at + ROW, :] = pltpu.roll(block, ROW - 2, 0).astype(BF16)
            tiles_x.append(block)
            tiles_g.append(jnp.concatenate([gbuf[:, j * PAIR : (j + 1) * PAIR].astype(F32), pad], axis=0))
        lanes = slice(pair * PAIR, (pair + 1) * PAIR)
        lhs_t[0:PAIR, lanes] = jnp.concatenate(tiles_x, axis=0).T.astype(BF16)
        lhs_t[PAIR : 2 * PAIR, lanes] = jnp.concatenate(tiles_g, axis=0).T.astype(BF16)

    def product(wanted, part):
        left = lhs_t[...] if part is None else lhs_t[part * PAIR : (part + 1) * PAIR, :]
        right = [shifted[d, (1 + s) * ROW : (1 + s) * ROW + rows, :] for d, s in wanted]
        full = jnp.dot(left, right[0] if len(right) == 1 else jnp.concatenate(right, axis=1), preferred_element_type=F32)
        return [full[:, k * PAIR : (k + 1) * PAIR] for k in range(len(right))]

    def table(at_s, base, s):
        upper = at_s[s][base : base + C, :]
        here = pltpu.roll(at_s[s][base + C : base + PAIR, :], C, 1)
        if s + 1 not in at_s:
            return upper + here
        after = pltpu.roll(at_s[s + 1][base + C : base + PAIR, :], C, 1)
        return upper + jnp.where(low, here, after)

    def odd(at_s, base, s):
        return at_s[s][base : base + C, :] + pltpu.roll(at_s[s + 1][base + C : base + PAIR, :], C, 1)

    def store(name, value):
        index = PLACE[name]
        slot = slot_of(index // QUART, layer, first, second)
        at = index % QUART * ROW
        out_ref[slot, at : at + ROW, :] = value

    row = lax.broadcasted_iota(jnp.int32, (ROW, PAIR), 0)
    col = lax.rem(lax.broadcasted_iota(jnp.int32, (ROW, PAIR), 1), C)
    pack = lambda a, b: jnp.where(row >= col, a, b)
    diagonal = lambda a: jnp.sum(jnp.where(row == col, a, 0.0), axis=0, keepdims=True)

    p = product(((0, -1), (0, 0)), 1) + product(((0, 1),), 1)
    at_s = dict(zip((-1, 0, 1), p))
    store("w0z", table(at_s, 0, 0))
    w0 = odd(at_s, 0, -1)
    same, under = product(((1, 1), (2, 1)), None)
    p = product(((1, -1), (1, 0)), None)
    at_s = dict(zip((-1, 0, 1), p + [same]))
    x0z = table(at_s, 0, 0)
    store("h0", jnp.where(low, table(at_s, 0, 1), w0))
    store("w1z", table(at_s, PAIR, 0))
    w1 = odd(at_s, PAIR, -1)
    p = product(((2, -1), (2, 0)), None)
    at_s = dict(zip((-1, 0, 1), p + [under]))
    store("x1m", table(at_s, 0, -1))
    store("x1z", table(at_s, 0, 0))
    x12 = table(at_s, 0, 1)
    store("w2z", table(at_s, PAIR, 0))
    w2 = odd(at_s, PAIR, -1)
    p = product(((3, -1), (3, 0)), 0) + product(((3, 1),), 0)
    at_s = dict(zip((-1, 0, 1), p))
    store("x2m", table(at_s, 0, -1))
    store("x2z", table(at_s, 0, 0))
    store("x22", jnp.where(low, x12, pltpu.roll(table(at_s, 0, 1), C, 1)))
    gl = lhs_t[PAIR : 2 * PAIR, :]
    gg = lax.dot_general(gl, gl, (((1,), (1,)), ((), ())), preferred_element_type=F32)
    gx = jnp.where(low, gg[0:C, :] + pltpu.roll(gg[C:PAIR, :], C, 1), pltpu.roll(x0z, C, 1))
    fl = [
        jnp.where(
            low,
            shifted[d, ROW : 2 * ROW, :].astype(F32),
            shifted[d, rows : ROW + rows, :].astype(F32),
        ).astype(BF16)
        for d in (1, 2, 3)
    ]
    for d, name in enumerate(("cg", "cc1", "cc2")):
        q = contract0(fl[0], fl[d])
        both = jnp.where(low, q[0:C, :], q[C:PAIR, :])
        if d == 0:
            name, both = "cg", pack(both, gx)
        store(name, both)
    line = lax.broadcasted_iota(jnp.int32, (n_edge, PAIR), 0)
    lane = lax.broadcasted_iota(jnp.int32, (n_edge, PAIR), 1)
    corner = ((line == 0) & (lane < C)) | ((line == wp - 1) & (lane >= C))
    halves = []
    lines = []
    corners = []
    for e in range(2):
        zero = edges[e, 8 : 8 + n_edge, :]
        here = zero.astype(BF16)
        after = edges[e, 9 : 9 + n_edge, :].astype(BF16)
        at_s = {0: contract0(here, here), 1: contract0(here, after)}
        lines.append(table(at_s, 0, 0))
        halves.append(table(at_s, 0, 1))
        only = jnp.where(corner, zero, 0.0).astype(BF16)
        q = contract0(only, only)
        corners.append(jnp.where(low, q[0:C, :], q[C:PAIR, :]))
    store("h1", jnp.where(low, halves[0], w1))
    store("h2", jnp.where(low, halves[1], w2))
    store("kk", pack(corners[0], corners[1]))
    store("r01", jnp.where(low, pltpu.roll(lines[0], C, 1), lines[1]))
    rx = jnp.where(low, pack(lines[0], lines[1]), x0z)
    diags = jnp.concatenate(
        [diagonal(corners[1]), diagonal(gx), diagonal(lines[1]), jnp.zeros((5, PAIR), F32)], axis=0
    )
    for quarter in range(4):
        slot = slot_of(quarter, layer, first, second)
        out_ref[slot, LAST:DIAGS, :] = rx[quarter * PIECE : (quarter + 1) * PIECE, :]
        out_ref[slot, DIAGS:QROWS, :] = diags
    if not own:
        copies[2].wait()
        copies[3].wait()


def local_sums(height, width, own, x, g):
    wp = width // 2
    sums = jax.ShapeDtypeStruct((4, QROWS, PAIR), F32)
    image = jax.ShapeDtypeStruct((height, width * C), BF16)
    n_edge = (wp + 15) // 16 * 16
    vmem = pl.BlockSpec(memory_space=pltpu.VMEM)
    scratch = [
        pltpu.VMEM((4, (wp + 2) * ROW, PAIR), BF16),
        pltpu.VMEM((2 * PAIR, wp * ROW), BF16),
        pltpu.VMEM((2, n_edge + 16, PAIR), F32),
    ]
    if not own:
        scratch = [pltpu.VMEM(image.shape, BF16)] * 2 + scratch + [pltpu.SemaphoreType.DMA((4,))]
    return pl.pallas_call(
        functools.partial(local_kernel, height, width, own),
        out_shape=sums if own else (sums, image, image),
        in_specs=[vmem if own else pl.BlockSpec(memory_space=pltpu.HBM)] * 2,
        out_specs=vmem if own else (vmem,) * 3,
        scratch_shapes=scratch,
        compiler_params=pltpu.CompilerParams(vmem_limit_bytes=SUMS_VMEM),
    )(x, g)


def split(a):
    high = a.astype(BF16)
    return high, (a - high.astype(F32)).astype(BF16)


def dot3(a, b):
    ah, al = split(a)
    bh, bl = split(b)
    dot = functools.partial(jnp.dot, preferred_element_type=F32)
    return dot(ah, bh) + (dot(ah, bl) + dot(al, bh))


def normalized(m):
    n = m.shape[0]
    diag = lax.broadcasted_iota(jnp.int32, (n, n), 0) == lax.broadcasted_iota(jnp.int32, (n, n), 1)
    trace = jnp.sum(jnp.where(diag, m, 0.0))
    m = m + jnp.where(diag, DAMP * trace / n, 0.0)
    inv = lax.rsqrt(jnp.sum(m * m))
    return jnp.where(diag, 1.0, 0.0) - m * inv, inv


def final_kernel(total_rows, own_ref, beside_ref, below_ref, across_ref, out_ref, quarters, m_hi, m_lo):
    _, first, second = chip_place()
    for slot, ref in enumerate((own_ref, beside_ref, below_ref, across_ref)):
        quarters[slot] = ref[...]

    def slot(quarter):
        return gathered_slot(quarter, first, second)

    def load(name):
        index = PLACE[name]
        at = index % QUART * ROW
        both = quarters[slot(index // QUART), at : at + ROW, :]
        return both[:, 0:C], both[:, C:PAIR]

    row = lax.broadcasted_iota(jnp.int32, (C, C), 0)
    col = lax.broadcasted_iota(jnp.int32, (C, C), 1)
    diags = quarters[slot(0), DIAGS:QROWS, :]

    def unpack(block, line, at):
        flipped = block.T
        mirrored = jnp.where(row < col, block, flipped)
        diagonal = jnp.broadcast_to(diags[line : line + 1, at : at + C], (C, C))
        return jnp.where(row >= col, block, flipped), jnp.where(row == col, diagonal, mirrored)

    rx = jnp.concatenate([quarters[slot(quarter), LAST:DIAGS, :] for quarter in range(4)], axis=0)
    x0 = {1: rx[:, C:PAIR]}
    row0 = {}
    row1 = {}
    col0 = {}
    col1 = {}
    row0[0], row1[0] = unpack(rx[:, 0:C], 2, 0)
    row0[1], row1[1] = load("r01")
    x0[2], w00 = load("h0")
    row0[2], w10 = load("h1")
    row1[2], w20 = load("h2")
    low, high = load("cg")
    col0[0], g = unpack(low, 1, 0)
    col1[0], x0[0] = unpack(high, 1, C)
    low, high = load("kk")
    k00, k10 = unpack(low, 0, 0)
    k01, k11 = unpack(high, 0, C)
    corner = (k00, k01, k10, k11)
    down = {}
    for dr in (1, 2):
        down[dr, -2], down[dr, -1] = load("x%dm" % dr)
        down[dr, 0], down[dr, 1] = load("x%dz" % dr)
        col0[dr], col1[dr] = load("cc%d" % dr)
    down[1, 2], down[2, 2] = load("x22")

    eg, inv_g = normalized(g)
    eg2 = dot3(eg, eg)
    pg = eg + dot3(eg, eg2) + eg2
    w0 = load("w0z")
    w1 = load("w1z")
    w2 = load("w2z")
    w = jnp.concatenate([w00, w0[0], w0[1], w10, w1[0], w1[1], w20, w2[0], w2[1]], axis=1)
    w = w + dot3(pg, w)
    w = w.T
    squares = []

    def put(t, u, block):
        high, rest = split(block)
        m_hi[t * C : (t + 1) * C, u * C : (u + 1) * C] = high
        m_lo[t * C : (t + 1) * C, u * C : (u + 1) * C] = rest

    def put_all(taps, block):
        squares.append(2.0 * len(taps) * (block * block))
        for t, u in taps:
            put(t, u, block)
        flipped = block.T
        for t, u in taps:
            put(u, t, flipped)

    on_diagonal = []
    for a in range(3):
        line = {}
        for dc in range(3):
            line[dc] = x0[dc] - row1[dc] if a == 0 else (x0[dc] - row0[dc] if a == 2 else x0[dc])
        for b in range(3):
            block = line[0]
            if b == 0:
                block = block - col1[0]
                if a == 0:
                    block = block + corner[3]
                if a == 2:
                    block = block + corner[1]
            if b == 2:
                block = block - col0[0]
                if a == 0:
                    block = block + corner[2]
                if a == 2:
                    block = block + corner[0]
            squares.append(block * block)
            on_diagonal.append(block)
            put(3 * a + b, 3 * a + b, block)
        put_all([(3 * a, 3 * a + 1), (3 * a + 1, 3 * a + 2)], line[1])
        put_all([(3 * a, 3 * a + 2)], line[2])
    for dr in (1, 2):
        starts = range(3 - dr)
        for b in range(3):
            block = down[dr, 0]
            if b == 0:
                block = block - col1[dr]
            if b == 2:
                block = block - col0[dr]
            put_all([(3 * a + b, 3 * (a + dr) + b) for a in starts], block)
        for dc in (-2, -1, 1, 2):
            taps = [(3 * a + b, 3 * (a + dr) + b + dc) for a in starts for b in range(3) if 0 <= b + dc < 3]
            put_all(taps, down[dr, dc])

    n = TAPS * C
    trace = jnp.sum(jnp.where(row == col, sum(on_diagonal), 0.0))
    shift = DAMP * trace / n
    inv_a = lax.rsqrt(jnp.sum(sum(squares)) + shift * (2.0 * trace + n * shift))
    keep = 1.0 - inv_a * shift
    v = w * (inv_a * inv_g * total_rows)

    def apply(v):
        vh, vl = split(v)
        both = jnp.dot(m_hi[...], jnp.concatenate([vh, vl], axis=1), preferred_element_type=F32)
        mv = both[:, 0:C] + (both[:, C:PAIR] + jnp.dot(m_lo[...], vh, preferred_element_type=F32))
        return keep * v - inv_a * mv

    v = v + apply(v)
    v = v + apply(apply(v))
    out_ref[...] = v.T


def precondition(parts, total_rows):
    n = TAPS * C
    return pl.pallas_call(
        functools.partial(final_kernel, float(total_rows)),
        out_shape=jax.ShapeDtypeStruct((C, n), F32),
        in_specs=[pl.BlockSpec(memory_space=pltpu.VMEM)] * 4,
        out_specs=pl.BlockSpec(memory_space=pltpu.VMEM),
        scratch_shapes=[
            pltpu.VMEM((4, QROWS, PAIR), F32),
            pltpu.VMEM((n, n), BF16),
            pltpu.VMEM((n, n), BF16),
        ],
        compiler_params=pltpu.CompilerParams(vmem_limit_bytes=VMEM_LIMIT),
    )(*parts)


def pairings(n_dp, n_grp):
    n = n_dp * n_grp
    core_bit = n_grp
    first, second = 1, 2 * n_grp
    doublings = []
    bit = 4 * n_grp
    while bit < n:
        doublings.append(bit)
        bit *= 2
    orders = ([first, second] + doublings, [second, first] + doublings[::-1])
    pairs = lambda masks: [(i, i ^ masks[1 if i & core_bit else 0]) for i in range(n)]
    rounds = [pairs(masks) for masks in zip(*orders)]
    return pairs((core_bit, core_bit)), rounds[:2], rounds[2:], (pairs((first, first)), pairs((second, second)), pairs((first + second, first + second)))


def shards(feature_maps, output_grads):
    n_dp, n_grp = lax.axis_size("dp"), lax.axis_size("grp")
    cores, halvings, doublings, gathers = pairings(n_dp, n_grp)
    swap = lambda a, p: lax.ppermute(a, ("dp", "grp"), p)
    total_rows = feature_maps.shape[2] * feature_maps.shape[3] // C * feature_maps.shape[1] * n_dp * n_grp
    height = feature_maps.shape[2]
    width = feature_maps.shape[3] // C
    send, own_x, own_g = local_sums(height, width, False, feature_maps, output_grads)
    got = swap(send, cores)
    keep = local_sums(height, width, True, own_x, own_g)
    far_next = swap(keep[3] + got[3], halvings[0])
    far_own = swap(keep[2] + got[2], halvings[0])
    got_next = swap(keep[1] + got[1] + far_next, halvings[1])
    own = keep[0] + got[0] + far_own + got_next
    for p in doublings:
        own = own + swap(own, p)
    beside = swap(own, gathers[0])
    below = swap(own, gathers[1])
    across = swap(own, gathers[2])
    mine = precondition((own, beside, below, across), total_rows)
    other = swap(mine, cores)
    core = lax.rem(lax.axis_index("dp"), 2)
    result = jnp.zeros((2,) + mine.shape, F32)
    result = lax.dynamic_update_slice(result, mine[None], (core, 0, 0))
    return lax.dynamic_update_slice(result, other[None], (1 - core, 0, 0))


def solution(mesh):
    placed = (P(None, ("dp", "grp"), None, None), P(None, ("dp", "grp"), None, None))
    return jax.shard_map(shards, mesh=mesh, in_specs=placed, out_specs=P(), check_vma=False)
```

```python
import functools

import jax
import jax.numpy as jnp
import numpy as np
from jax import lax
from jax.experimental import pallas as pl
from jax.experimental.pallas import tpu as pltpu
from jax.sharding import PartitionSpec as P

C = 64
TAPS = 9
PAIR = 2 * C
ROW = 64
QUART = 4
DAMP = 0.1
SUMS_VMEM = 52 * 2**20
VMEM_LIMIT = 48 * 2**20
F32 = jnp.float32
BF16 = jnp.bfloat16

PAIRS = (
    "x1m", "x1z", "cc1", "x2m",
    "x2z", "cc2", "x22", "kk",
    "cg", "w0z", "w1z", "w2z",
    "h0", "h1", "h2", "r01",
)
PLACE = {name: index for index, name in enumerate(PAIRS)}
LAST = QUART * ROW
PIECE = ROW // 4
DIAGS = LAST + PIECE
QROWS = DIAGS + 8


def contract0(a, b):
    return lax.dot_general(a, b, (((0,), (0,)), ((), ())), preferred_element_type=F32)


def chip_place():
    dp = lax.axis_index("dp")
    core = lax.rem(dp, 2)
    second = lax.rem(dp // 2, 2)
    first = lax.axis_index("grp")
    return core, first, second


def slot_of(quarter, layer, first, second):
    mine_first = first ^ (quarter // 2)
    mine_second = second ^ (quarter % 2)
    major = jnp.where(layer == 0, mine_first, mine_second)
    minor = jnp.where(layer == 0, mine_second, mine_first)
    return 2 * major + minor


def gathered_slot(quarter, first, second):
    return 2 * (second ^ (quarter % 2)) + (first ^ (quarter // 2))


def local_kernel(height, width, own, *refs):
    if own:
        xbuf, gbuf, out_ref, shifted, lhs_t, edges = refs
    else:
        x_hbm, g_hbm, out_ref, next_x, next_g, xbuf, gbuf, shifted, lhs_t, edges, sems = refs
    core, first, second = chip_place()
    wp = width // 2
    rows = wp * ROW
    layer = core if own else 1 - core
    if not own:
        copies = [
            pltpu.make_async_copy(x_hbm.at[layer, 0], xbuf, sems.at[0]),
            pltpu.make_async_copy(g_hbm.at[layer, 0], gbuf, sems.at[1]),
            pltpu.make_async_copy(x_hbm.at[core, 0], next_x, sems.at[2]),
            pltpu.make_async_copy(g_hbm.at[core, 0], next_g, sems.at[3]),
        ]
        for one in copies:
            one.start()
    for d in range(4):
        shifted[d, 0:ROW, :] = jnp.zeros((ROW, PAIR), BF16)
        shifted[d, ROW + rows : 2 * ROW + rows, :] = jnp.zeros((ROW, PAIR), BF16)
    edges[...] = jnp.zeros_like(edges)
    low = lax.broadcasted_iota(jnp.int32, (ROW, PAIR), 1) < C
    pad = jnp.zeros((ROW - height, PAIR), F32)
    n_edge = edges.shape[1] - 16
    if not own:
        copies[0].wait()
    for pair in range(wp // 2):
        tiles_x = []
        for half in range(2):
            j = 2 * pair + half
            block = jnp.concatenate([xbuf[:, j * PAIR : (j + 1) * PAIR].astype(F32), pad], axis=0)
            at = ROW + j * ROW
            edges[0, 8 + j : 9 + j, :] = block[0:1, :]
            edges[1, 8 + j : 9 + j, :] = block[height - 1 : height, :]
            shifted[0, at : at + ROW, :] = pltpu.roll(block, 1, 0).astype(BF16)
            shifted[1, at : at + ROW, :] = block.astype(BF16)
            shifted[2, at : at + ROW, :] = pltpu.roll(block, ROW - 1, 0).astype(BF16)
            shifted[3, at : at + ROW, :] = pltpu.roll(block, ROW - 2, 0).astype(BF16)
            tiles_x.append(block)
        lanes = slice(pair * PAIR, (pair + 1) * PAIR)
        lhs_t[0:PAIR, lanes] = jnp.concatenate(tiles_x, axis=0).T.astype(BF16)
    if not own:
        copies[1].wait()
    for pair in range(wp // 2):
        tiles_g = []
        for j in (2 * pair, 2 * pair + 1):
            tiles_g.append(jnp.concatenate([gbuf[:, j * PAIR : (j + 1) * PAIR].astype(F32), pad], axis=0))
        lanes = slice(pair * PAIR, (pair + 1) * PAIR)
        lhs_t[PAIR : 2 * PAIR, lanes] = jnp.concatenate(tiles_g, axis=0).T.astype(BF16)

    def product(wanted, part):
        left = lhs_t[...] if part is None else lhs_t[part * PAIR : (part + 1) * PAIR, :]
        right = [shifted[d, (1 + s) * ROW : (1 + s) * ROW + rows, :] for d, s in wanted]
        full = jnp.dot(left, right[0] if len(right) == 1 else jnp.concatenate(right, axis=1), preferred_element_type=F32)
        return [full[:, k * PAIR : (k + 1) * PAIR] for k in range(len(right))]

    def table(at_s, base, s):
        upper = at_s[s][base : base + C, :]
        here = pltpu.roll(at_s[s][base + C : base + PAIR, :], C, 1)
        if s + 1 not in at_s:
            return upper + here
        after = pltpu.roll(at_s[s + 1][base + C : base + PAIR, :], C, 1)
        return upper + jnp.where(low, here, after)

    def odd(at_s, base, s):
        return at_s[s][base : base + C, :] + pltpu.roll(at_s[s + 1][base + C : base + PAIR, :], C, 1)

    def store(name, value):
        index = PLACE[name]
        slot = slot_of(index // QUART, layer, first, second)
        at = index % QUART * ROW
        out_ref[slot, at : at + ROW, :] = value

    row = lax.broadcasted_iota(jnp.int32, (ROW, PAIR), 0)
    col = lax.rem(lax.broadcasted_iota(jnp.int32, (ROW, PAIR), 1), C)
    pack = lambda a, b: jnp.where(row >= col, a, b)
    diagonal = lambda a: jnp.sum(jnp.where(row == col, a, 0.0), axis=0, keepdims=True)

    p = product(((0, -1), (0, 0)), 1) + product(((0, 1),), 1)
    at_s = dict(zip((-1, 0, 1), p))
    store("w0z", table(at_s, 0, 0))
    w0 = odd(at_s, 0, -1)
    same, under = product(((1, 1), (2, 1)), None)
    p = product(((1, -1), (1, 0)), None)
    at_s = dict(zip((-1, 0, 1), p + [same]))
    x0z = table(at_s, 0, 0)
    store("h0", jnp.where(low, table(at_s, 0, 1), w0))
    store("w1z", table(at_s, PAIR, 0))
    w1 = odd(at_s, PAIR, -1)
    p = product(((2, -1), (2, 0)), None)
    at_s = dict(zip((-1, 0, 1), p + [under]))
    store("x1m", table(at_s, 0, -1))
    store("x1z", table(at_s, 0, 0))
    x12 = table(at_s, 0, 1)
    store("w2z", table(at_s, PAIR, 0))
    w2 = odd(at_s, PAIR, -1)
    p = product(((3, -1), (3, 0)), 0) + product(((3, 1),), 0)
    at_s = dict(zip((-1, 0, 1), p))
    store("x2m", table(at_s, 0, -1))
    store("x2z", table(at_s, 0, 0))
    store("x22", jnp.where(low, x12, pltpu.roll(table(at_s, 0, 1), C, 1)))
    gl = lhs_t[PAIR : 2 * PAIR, :]
    gg = lax.dot_general(gl, gl, (((1,), (1,)), ((), ())), preferred_element_type=F32)
    gx = jnp.where(low, gg[0:C, :] + pltpu.roll(gg[C:PAIR, :], C, 1), pltpu.roll(x0z, C, 1))
    fl = [
        jnp.where(
            low,
            shifted[d, ROW : 2 * ROW, :].astype(F32),
            shifted[d, rows : ROW + rows, :].astype(F32),
        ).astype(BF16)
        for d in (1, 2, 3)
    ]
    for d, name in enumerate(("cg", "cc1", "cc2")):
        q = contract0(fl[0], fl[d])
        both = jnp.where(low, q[0:C, :], q[C:PAIR, :])
        if d == 0:
            name, both = "cg", pack(both, gx)
        store(name, both)
    line = lax.broadcasted_iota(jnp.int32, (n_edge, PAIR), 0)
    lane = lax.broadcasted_iota(jnp.int32, (n_edge, PAIR), 1)
    corner = ((line == 0) & (lane < C)) | ((line == wp - 1) & (lane >= C))
    halves = []
    lines = []
    corners = []
    for e in range(2):
        zero = edges[e, 8 : 8 + n_edge, :]
        here = zero.astype(BF16)
        after = edges[e, 9 : 9 + n_edge, :].astype(BF16)
        at_s = {0: contract0(here, here), 1: contract0(here, after)}
        lines.append(table(at_s, 0, 0))
        halves.append(table(at_s, 0, 1))
        only = jnp.where(corner, zero, 0.0).astype(BF16)
        q = contract0(only, only)
        corners.append(jnp.where(low, q[0:C, :], q[C:PAIR, :]))
    store("h1", jnp.where(low, halves[0], w1))
    store("h2", jnp.where(low, halves[1], w2))
    store("kk", pack(corners[0], corners[1]))
    store("r01", jnp.where(low, pltpu.roll(lines[0], C, 1), lines[1]))
    rx = jnp.where(low, pack(lines[0], lines[1]), x0z)
    diags = jnp.concatenate(
        [diagonal(corners[1]), diagonal(gx), diagonal(lines[1]), jnp.zeros((5, PAIR), F32)], axis=0
    )
    for quarter in range(4):
        slot = slot_of(quarter, layer, first, second)
        out_ref[slot, LAST:DIAGS, :] = rx[quarter * PIECE : (quarter + 1) * PIECE, :]
        out_ref[slot, DIAGS:QROWS, :] = diags
    if not own:
        copies[2].wait()
        copies[3].wait()


def local_sums(height, width, own, x, g):
    wp = width // 2
    sums = jax.ShapeDtypeStruct((4, QROWS, PAIR), F32)
    image = jax.ShapeDtypeStruct((height, width * C), BF16)
    n_edge = (wp + 15) // 16 * 16
    vmem = pl.BlockSpec(memory_space=pltpu.VMEM)
    scratch = [
        pltpu.VMEM((4, (wp + 2) * ROW, PAIR), BF16),
        pltpu.VMEM((2 * PAIR, wp * ROW), BF16),
        pltpu.VMEM((2, n_edge + 16, PAIR), F32),
    ]
    if not own:
        scratch = [pltpu.VMEM(image.shape, BF16)] * 2 + scratch + [pltpu.SemaphoreType.DMA((4,))]
    return pl.pallas_call(
        functools.partial(local_kernel, height, width, own),
        out_shape=sums if own else (sums, image, image),
        in_specs=[vmem if own else pl.BlockSpec(memory_space=pltpu.HBM)] * 2,
        out_specs=vmem if own else (vmem,) * 3,
        scratch_shapes=scratch,
        compiler_params=pltpu.CompilerParams(vmem_limit_bytes=SUMS_VMEM),
    )(x, g)


def split(a):
    high = a.astype(BF16)
    return high, (a - high.astype(F32)).astype(BF16)


def dot3(a, b):
    ah, al = split(a)
    bh, bl = split(b)
    dot = functools.partial(jnp.dot, preferred_element_type=F32)
    return dot(ah, bh) + (dot(ah, bl) + dot(al, bh))


def normalized(m):
    n = m.shape[0]
    diag = lax.broadcasted_iota(jnp.int32, (n, n), 0) == lax.broadcasted_iota(jnp.int32, (n, n), 1)
    trace = jnp.sum(jnp.where(diag, m, 0.0))
    m = m + jnp.where(diag, DAMP * trace / n, 0.0)
    inv = lax.rsqrt(jnp.sum(m * m))
    return jnp.where(diag, 1.0, 0.0) - m * inv, inv


def final_kernel(total_rows, own_ref, beside_ref, below_ref, across_ref, out_ref, quarters, m_hi, m_lo):
    _, first, second = chip_place()
    for slot, ref in enumerate((own_ref, beside_ref, below_ref, across_ref)):
        quarters[slot] = ref[...]

    def slot(quarter):
        return gathered_slot(quarter, first, second)

    def load(name):
        index = PLACE[name]
        at = index % QUART * ROW
        both = quarters[slot(index // QUART), at : at + ROW, :]
        return both[:, 0:C], both[:, C:PAIR]

    row = lax.broadcasted_iota(jnp.int32, (C, C), 0)
    col = lax.broadcasted_iota(jnp.int32, (C, C), 1)
    diags = quarters[slot(0), DIAGS:QROWS, :]

    def unpack(block, line, at):
        flipped = block.T
        mirrored = jnp.where(row < col, block, flipped)
        diagonal = jnp.broadcast_to(diags[line : line + 1, at : at + C], (C, C))
        return jnp.where(row >= col, block, flipped), jnp.where(row == col, diagonal, mirrored)

    rx = jnp.concatenate([quarters[slot(quarter), LAST:DIAGS, :] for quarter in range(4)], axis=0)
    x0 = {1: rx[:, C:PAIR]}
    row0 = {}
    row1 = {}
    col0 = {}
    col1 = {}
    row0[0], row1[0] = unpack(rx[:, 0:C], 2, 0)
    row0[1], row1[1] = load("r01")
    x0[2], w00 = load("h0")
    row0[2], w10 = load("h1")
    row1[2], w20 = load("h2")
    low, high = load("cg")
    col0[0], g = unpack(low, 1, 0)
    col1[0], x0[0] = unpack(high, 1, C)
    low, high = load("kk")
    k00, k10 = unpack(low, 0, 0)
    k01, k11 = unpack(high, 0, C)
    corner = (k00, k01, k10, k11)
    down = {}
    for dr in (1, 2):
        down[dr, -2], down[dr, -1] = load("x%dm" % dr)
        down[dr, 0], down[dr, 1] = load("x%dz" % dr)
        col0[dr], col1[dr] = load("cc%d" % dr)
    down[1, 2], down[2, 2] = load("x22")

    eg, inv_g = normalized(g)
    eg2 = dot3(eg, eg)
    pg = eg + dot3(eg, eg2) + eg2
    w0 = load("w0z")
    w1 = load("w1z")
    w2 = load("w2z")
    w = jnp.concatenate([w00, w0[0], w0[1], w10, w1[0], w1[1], w20, w2[0], w2[1]], axis=1)
    w = w + dot3(pg, w)
    w = w.T
    squares = []

    def put(t, u, block):
        high, rest = split(block)
        m_hi[t * C : (t + 1) * C, u * C : (u + 1) * C] = high
        m_lo[t * C : (t + 1) * C, u * C : (u + 1) * C] = rest

    def put_all(taps, block):
        squares.append(2.0 * len(taps) * (block * block))
        for t, u in taps:
            put(t, u, block)
        flipped = block.T
        for t, u in taps:
            put(u, t, flipped)

    on_diagonal = []
    for a in range(3):
        line = {}
        for dc in range(3):
            line[dc] = x0[dc] - row1[dc] if a == 0 else (x0[dc] - row0[dc] if a == 2 else x0[dc])
        for b in range(3):
            block = line[0]
            if b == 0:
                block = block - col1[0]
                if a == 0:
                    block = block + corner[3]
                if a == 2:
                    block = block + corner[1]
            if b == 2:
                block = block - col0[0]
                if a == 0:
                    block = block + corner[2]
                if a == 2:
                    block = block + corner[0]
            squares.append(block * block)
            on_diagonal.append(block)
            put(3 * a + b, 3 * a + b, block)
        put_all([(3 * a, 3 * a + 1), (3 * a + 1, 3 * a + 2)], line[1])
        put_all([(3 * a, 3 * a + 2)], line[2])
    for dr in (1, 2):
        starts = range(3 - dr)
        for b in range(3):
            block = down[dr, 0]
            if b == 0:
                block = block - col1[dr]
            if b == 2:
                block = block - col0[dr]
            put_all([(3 * a + b, 3 * (a + dr) + b) for a in starts], block)
        for dc in (-2, -1, 1, 2):
            taps = [(3 * a + b, 3 * (a + dr) + b + dc) for a in starts for b in range(3) if 0 <= b + dc < 3]
            put_all(taps, down[dr, dc])

    n = TAPS * C
    trace = jnp.sum(jnp.where(row == col, sum(on_diagonal), 0.0))
    shift = DAMP * trace / n
    inv_a = lax.rsqrt(jnp.sum(sum(squares)) + shift * (2.0 * trace + n * shift))
    keep = 1.0 - inv_a * shift
    v = w * (inv_a * inv_g * total_rows)

    def apply(v):
        vh, vl = split(v)
        both = jnp.dot(m_hi[...], jnp.concatenate([vh, vl], axis=1), preferred_element_type=F32)
        mv = both[:, 0:C] + (both[:, C:PAIR] + jnp.dot(m_lo[...], vh, preferred_element_type=F32))
        return keep * v - inv_a * mv

    v = v + apply(v)
    v = v + apply(apply(v))
    out_ref[...] = v.T


def precondition(parts, total_rows):
    n = TAPS * C
    return pl.pallas_call(
        functools.partial(final_kernel, float(total_rows)),
        out_shape=jax.ShapeDtypeStruct((C, n), F32),
        in_specs=[pl.BlockSpec(memory_space=pltpu.VMEM)] * 4,
        out_specs=pl.BlockSpec(memory_space=pltpu.VMEM),
        scratch_shapes=[
            pltpu.VMEM((4, QROWS, PAIR), F32),
            pltpu.VMEM((n, n), BF16),
            pltpu.VMEM((n, n), BF16),
        ],
        compiler_params=pltpu.CompilerParams(vmem_limit_bytes=VMEM_LIMIT),
    )(*parts)


def pairings(n_dp, n_grp):
    n = n_dp * n_grp
    core_bit = n_grp
    first, second = 1, 2 * n_grp
    doublings = []
    bit = 4 * n_grp
    while bit < n:
        doublings.append(bit)
        bit *= 2
    orders = ([first, second] + doublings, [second, first] + doublings[::-1])
    pairs = lambda masks: [(i, i ^ masks[1 if i & core_bit else 0]) for i in range(n)]
    rounds = [pairs(masks) for masks in zip(*orders)]
    return pairs((core_bit, core_bit)), rounds[:2], rounds[2:], (pairs((first, first)), pairs((second, second)), pairs((first + second, first + second)))


def shards(feature_maps, output_grads):
    n_dp, n_grp = lax.axis_size("dp"), lax.axis_size("grp")
    cores, halvings, doublings, gathers = pairings(n_dp, n_grp)
    swap = lambda a, p: lax.ppermute(a, ("dp", "grp"), p)
    total_rows = feature_maps.shape[2] * feature_maps.shape[3] // C * feature_maps.shape[1] * n_dp * n_grp
    height = feature_maps.shape[2]
    width = feature_maps.shape[3] // C
    send, own_x, own_g = local_sums(height, width, False, feature_maps, output_grads)
    got = swap(send, cores)
    keep = local_sums(height, width, True, own_x, own_g)
    far_next = swap(keep[3] + got[3], halvings[0])
    far_own = swap(keep[2] + got[2], halvings[0])
    got_next = swap(keep[1] + got[1] + far_next, halvings[1])
    own = keep[0] + got[0] + far_own + got_next
    for p in doublings:
        own = own + swap(own, p)
    beside = swap(own, gathers[0])
    below = swap(own, gathers[1])
    across = swap(own, gathers[2])
    mine = precondition((own, beside, below, across), total_rows)
    other = swap(mine, cores)
    core = lax.rem(lax.axis_index("dp"), 2)
    result = jnp.zeros((2,) + mine.shape, F32)
    result = lax.dynamic_update_slice(result, mine[None], (core, 0, 0))
    return lax.dynamic_update_slice(result, other[None], (1 - core, 0, 0))


def solution(mesh):
    placed = (P(None, ("dp", "grp"), None, None), P(None, ("dp", "grp"), None, None))
    return jax.shard_map(shards, mesh=mesh, in_specs=placed, out_specs=P(), check_vma=False)
```
